128 devices in a mesh: row: 16 (over y_lo, z, core), col: 8 (over x, y_hi).
Axes of the slice: x: 4, y: 4 (y_hi: 2, y_lo: 2; y = y_hi * 2 + y_lo), z: 4, core: 2. Of those that a mesh axis runs over, the one named last changes fastest.
Arguments:
- alignment: bfloat16 [256, 32768], P('row', 'col'), may hold values from -6 to 6
- pair_state: float32 [512, 512, 128], P('row', 'col'), may hold values from -6 to 6
- alignment_factor_weight: bfloat16 [64, 64], replicated, may hold values from -0.75 to 0.75
- outer_proj: bfloat16 [1024, 128], replicated, may hold values from -3 to 3
- outgoing_proj: bfloat16 [128, 640], replicated, may hold values from -0.5 to 0.5
- outgoing_final: bfloat16 [128, 128], replicated, may hold values from -0.5 to 0.5
- incoming_proj: bfloat16 [128, 640], replicated, may hold values from -0.5 to 0.5
- incoming_final: bfloat16 [128, 128], replicated, may hold values from -0.5 to 0.5
Outputs:
- pair_result: float32 [512, 512, 128], P('row', 'col')
The draws below stay inside these ranges and needn't reach their ends.
All inputs are finite; a program needn't handle non-finite values.
Results may differ from the reference program's by a relative error of at most 0.0065.
Values may be sent and summed in bfloat16 or wider, within the bound.
A program may use at most 128 MiB of HBM per device.

```python
import jax
import jax.numpy as jnp
from jax import lax

C = 128
CM = 64
CH = 32
CT = 128
S = 256
TOKENS_PER_ROW = 32
N = 512


def steps_of(rng, dims, pieces, low, high):
    gain, own = 1.0, jax.random.fold_in(rng, 6)
    for axis_at, shards_of in pieces:
        steps = jnp.exp(jax.random.uniform(jax.random.fold_in(own, axis_at), (shards_of,), jnp.float32, low / len(pieces), high / len(pieces)))
        gain = gain * jnp.repeat(steps, dims[axis_at] // shards_of).reshape([-1 if axis == axis_at else 1 for axis in range(len(dims))])
    return gain


def gaussian(rng, dims, scale, limit, cuts=(), kind=jnp.bfloat16):
    drawn = jax.random.normal(rng, dims, jnp.float32) * scale
    if len(cuts) > 0:
        drawn = steps_of(rng, dims, cuts, -0.22, 0.18) * drawn
    return jnp.clip(drawn, min=-limit, max=limit).astype(kind)


def setup_inputs(seed: int = 0) -> dict:
    key_list = jax.random.split(jax.random.key(seed), 9)
    return {
        "alignment": gaussian(key_list[0], (S, N * CM), 1.0, 6.0, ((0, 16), (1, 8))),
        "pair_state": gaussian(key_list[1], (N, N, C), 1.0, 6.0, ((0, 16), (1, 8)), jnp.float32),
        "alignment_factor_weight": gaussian(key_list[2], (CM, 2 * CH), CM ** -0.5, 0.75),
        "outer_proj": gaussian(key_list[3], (CH * CH, C), (max(1, CH * CH // S)) ** -0.5, 3.0),
        "outgoing_proj": gaussian(key_list[4], (C, 4 * CT + C), C ** -0.5, 0.5),
        "outgoing_final": gaussian(key_list[5], (CT, C), CT ** -0.5, 0.5),
        "incoming_proj": gaussian(key_list[6], (C, 4 * CT + C), C ** -0.5, 0.5),
        "incoming_final": gaussian(key_list[7], (CT, C), CT ** -0.5, 0.5),
    }


epsilon = 1e-05

def normalize_layer(values):
    average = lax.optimization_barrier(jnp.mean(values, axis=-1, keepdims=True))
    centred = values - average
    spread = lax.optimization_barrier(jnp.mean(centred * centred, axis=-1, keepdims=True))
    return centred * lax.rsqrt(spread + epsilon)

def triangle(pair_now, weights, final_weights, outgoing):
    hidden_dim = final_weights.shape[0]
    channels = pair_now.shape[-1]
    tokens = pair_now.shape[0]
    normed_in = normalize_layer(pair_now).astype(jnp.bfloat16).reshape(-1, channels)

    def project_cols(begin_col, end_col):
        result = jnp.dot(normed_in, weights[:, begin_col:end_col], preferred_element_type=jnp.float32)
        return result.reshape(tokens, tokens, end_col - begin_col)
    left_factor = (jax.nn.sigmoid(project_cols(0, hidden_dim)) * project_cols(hidden_dim, 2 * hidden_dim)).astype(jnp.bfloat16)
    right_factor = (jax.nn.sigmoid(project_cols(2 * hidden_dim, 3 * hidden_dim)) * project_cols(3 * hidden_dim, 4 * hidden_dim)).astype(jnp.bfloat16)
    gate_vals = jax.nn.sigmoid(project_cols(4 * hidden_dim, 4 * hidden_dim + channels))
    left_wide = left_factor.astype(jnp.float32)
    right_wide = right_factor.astype(jnp.float32)
    if outgoing:
        mixed_sum = jnp.einsum('ikc,jkc->ijc', left_wide, right_wide, precision=lax.Precision.HIGHEST)
    else:
        mixed_sum = jnp.einsum('kic,kjc->ijc', left_wide, right_wide, precision=lax.Precision.HIGHEST)
    normed_mix = normalize_layer(mixed_sum).astype(jnp.bfloat16).reshape(-1, hidden_dim)
    update = jnp.dot(normed_mix, final_weights, preferred_element_type=jnp.float32).reshape(tokens, tokens, channels)
    return pair_now + gate_vals * update

def reference(alignment, pair_state, alignment_factor_weight, outer_proj, outgoing_proj, outgoing_final, incoming_proj, incoming_final):
    tokens = pair_state.shape[0]
    seq_count = alignment.shape[0]
    feature_width = alignment_factor_weight.shape[0]
    hidden_outer = alignment_factor_weight.shape[1] // 2
    feature_values = alignment.astype(jnp.float32).reshape(seq_count, tokens, feature_width)
    normalized_alignment = normalize_layer(feature_values).astype(jnp.bfloat16).reshape(-1, feature_width)
    factor_pairs = jnp.dot(normalized_alignment, alignment_factor_weight, preferred_element_type=jnp.float32).astype(jnp.bfloat16)
    factor_pairs = factor_pairs.reshape(seq_count, tokens, 2 * hidden_outer)
    row_factor = factor_pairs[:, :, :hidden_outer].reshape(seq_count, tokens * hidden_outer)
    col_factor = factor_pairs[:, :, hidden_outer:].reshape(seq_count, tokens * hidden_outer)
    block_rows = TOKENS_PER_ROW
    block_count = tokens // block_rows

    def one_block(block_index):
        row_part = lax.dynamic_slice_in_dim(row_factor, block_index * (block_rows * hidden_outer), block_rows * hidden_outer, 1)
        outer_sum = jnp.dot(row_part.T, col_factor, preferred_element_type=jnp.float32) / seq_count
        outer_mean = outer_sum.astype(jnp.bfloat16).reshape(block_rows, hidden_outer, tokens, hidden_outer)
        outer_mean = outer_mean.transpose(0, 2, 1, 3).reshape(block_rows * tokens, hidden_outer * hidden_outer)
        return jnp.dot(outer_mean, outer_proj, preferred_element_type=jnp.float32).reshape(block_rows, tokens, -1)
    opm_term = lax.map(one_block, jnp.arange(block_count, dtype=jnp.int32)).reshape(tokens, tokens, -1)
    pair_opm = pair_state + opm_term
    pair_mid = triangle(pair_opm, outgoing_proj, outgoing_final, True)
    return triangle(pair_mid, incoming_proj, incoming_final, False)
```

```python
import functools

import jax
import jax.numpy as jnp
from jax import lax
from jax.experimental import pallas as pl
from jax.experimental.pallas import tpu as pltpu
from jax.sharding import PartitionSpec as P

epsilon = 1e-05
MESH = pl.DeviceIdType.MESH
NR, NC = 16, 8
ND = NR * NC
BF, F32 = jnp.bfloat16, jnp.float32


def sigmoid(x):
    return 0.5 * jnp.tanh(0.5 * x) + 0.5


def position():
    r, c = lax.axis_index("row"), lax.axis_index("col")
    return r, c, c // 2, lax.rem(c, 2) * 2 + r // 8, lax.rem(r // 2, 4), lax.rem(r, 2)


def partner(where, step):
    _, _, x, y, z, core = where
    k = lax.rem(step * 107, ND)
    x = lax.rem(x + lax.rem(k // 2, 4), 4)
    y = lax.rem(y + lax.rem(k // 8, 4), 4)
    z = lax.rem(z + k // 32, 4)
    core = lax.rem(core + k, 2)
    return lax.rem(y, 2) * 8 + z * 2 + core, x * 2 + y // 2


def columns_normed(v):
    centred = v - jnp.mean(v, axis=0, keepdims=True)
    spread = jnp.mean(centred * centred, axis=0, keepdims=True)
    return centred * lax.rsqrt(spread + epsilon)


def exchange(where, source, target, sems):
    r, c = where[:2]
    me = r * NC + c

    def send(step, carry):
        rr, cc = partner(where, step)
        pltpu.make_async_remote_copy(
            source.at[rr * NC + cc],
            target.at[me],
            sems.at[0],
            sems.at[1],
            device_id=(rr, cc),
            device_id_type=MESH,
        ).start()
        return carry

    lax.fori_loop(1, ND, send, 0)
    target[me] = source[me]


def await_exchange(where, source, target, sems):
    pltpu.make_async_remote_copy(
        source.at[pl.ds(0, ND - 1)],
        target.at[pl.ds(0, ND - 1)],
        sems.at[0],
        sems.at[1],
        device_id=where[:2],
        device_id_type=MESH,
    ).wait()


def kernel(
    col_ref, row_ref, pair_ref, opm_w, out_w, out_f, in_w, in_f, result,
    col_all, row_all, row_t, outer, pair, gate, spread_l, spread_r, matrices,
    send1, got1, back1, mix1, send2, got2, back2, mix2, bsems, sems,
):
    where = position()
    r, c = where[:2]
    me = r * NC + c
    home = (r // 2 == c).astype(jnp.int32)
    bar = pltpu.get_barrier_semaphore()

    def greet(rr, cc):
        @pl.when(jnp.logical_or(rr != r, cc != c))
        def _():
            pl.semaphore_signal(bar, inc=1, device_id=(rr, cc), device_id_type=MESH)

    def greet_rows(k, carry):
        rr = lax.rem(r + k, NR)
        greet(rr, c)
        greet(rr, r // 2)
        return carry

    def greet_cols(k, carry):
        greet(r, lax.rem(c + k, NC))
        return carry

    lax.fori_loop(0, NR, greet_rows, 0)
    lax.fori_loop(1, NC, greet_cols, 0)
    pl.semaphore_wait(bar, (NR - 1) + (NC - 1) + NR - home)

    mine = pl.ds(pl.multiple_of(r * 16, 16), 16)

    def send_col(k, carry):
        pltpu.make_async_remote_copy(
            col_ref, col_all.at[mine], bsems.at[0], bsems.at[1],
            device_id=(lax.rem(r + k, NR), c), device_id_type=MESH,
        ).start()
        return carry

    def send_row(k, carry):
        half, cc = lax.rem(k, 2), lax.rem(c + k // 2, NC)
        rr = 2 * c + half

        @pl.when(jnp.logical_or(rr != r, cc != c))
        def _():
            pltpu.make_async_remote_copy(
                row_ref.at[half], row_all.at[mine], bsems.at[2], bsems.at[3],
                device_id=(rr, cc), device_id_type=MESH,
            ).start()

        return carry

    lax.fori_loop(0, NR, send_row, 0)
    lax.fori_loop(1, NR, send_col, 0)
    col_all[mine] = col_ref[...]

    @pl.when(home == 1)
    def _():
        row_all[mine] = row_ref[lax.rem(r, 2)]

    def turn(t, carry):
        block = jnp.concatenate([pair_ref[t], pair_ref[t + 16]], axis=0)
        pair[:, pl.ds(pl.multiple_of(t * 128, 128), 128)] = block.T
        return carry

    lax.fori_loop(0, 16, turn, 0)

    @pl.when(home == 1)
    def _():
        part = pl.ds(0, 15 * 16)
        pltpu.make_async_remote_copy(
            row_all.at[part], row_all.at[part], bsems.at[2], bsems.at[3],
            device_id=(r, c), device_id_type=MESH,
        ).wait()

    @pl.when(home == 0)
    def _():
        pltpu.make_async_remote_copy(
            row_all, row_all, bsems.at[2], bsems.at[3],
            device_id=(r, c), device_id_type=MESH,
        ).wait()

    row_t[...] = row_all[...].T
    part = pl.ds(0, 15 * 16)
    pltpu.make_async_remote_copy(
        col_all.at[part], col_all.at[part], bsems.at[0], bsems.at[1],
        device_id=(r, c), device_id_type=MESH,
    ).wait()

    def outer_part(n, carry):
        at = pl.ds(pl.multiple_of(n * 256, 256), 256)
        outer[:, at] = jnp.dot(row_t[...], col_all[:, at], preferred_element_type=F32).astype(BF)
        return carry

    lax.fori_loop(0, 8, outer_part, 0)

    def opm(t2, carry):
        sides = []
        for k in range(2):
            t = t2 * 2 + k
            low = outer[pl.ds(pl.multiple_of(t * 32, 32), 32), :]
            high = outer[pl.ds(pl.multiple_of(t * 32 + 512, 32), 32), :]
            evens, odds = [], []
            for q in range(16):
                a, b = low[:, q * 128 : q * 128 + 128], high[:, q * 128 : q * 128 + 128]
                evens.append(jnp.concatenate([a[:, :64], b[:, :64]], axis=1))
                odds.append(jnp.concatenate([a[:, 64:], b[:, 64:]], axis=1))
            sides.append(jnp.concatenate(evens + odds, axis=0))
        term = jnp.dot(opm_w[...], jnp.concatenate(sides, axis=1), preferred_element_type=F32)
        at = pl.ds(pl.multiple_of(t2 * 256, 256), 256)
        pair[:, at] += term * (1.0 / 256.0)
        return carry

    lax.fori_loop(0, 8, opm, 0)

    def project(weights, send):
        def one(t2, carry):
            at = pl.ds(pl.multiple_of(t2 * 256, 256), 256)
            normed = columns_normed(pair[:, at]).astype(BF)
            p = jnp.dot(weights[...], normed, preferred_element_type=F32)
            left = sigmoid(p[:128]) * p[128:256]
            right = sigmoid(p[256:384]) * p[384:512]
            gate[:, at] = sigmoid(p[512:])
            for k in range(2):
                for b in range(16):
                    to = pl.ds(b * 128 + t2 * 2 + k, 8, stride=16)
                    spread_l[to, :] = left[b * 8 : b * 8 + 8, k * 128 : k * 128 + 128]
                    spread_r[to, :] = right[b * 8 : b * 8 + 8, k * 128 : k * 128 + 128]
            return carry

        lax.fori_loop(0, 8, one, 0)

        def pack(n, carry):
            at = pl.ds(pl.multiple_of(n * 256, 256), 256)
            to = pl.ds(pl.multiple_of(n * 16, 16), 16)
            send[to, 0] = spread_l[at, :].astype(BF).reshape(16, 16, 128)
            send[to, 1] = spread_r[at, :].astype(BF).reshape(16, 16, 128)
            return carry

        lax.fori_loop(0, 8, pack, 0)

    def mix(got, back, outgoing):
        for f in range(2):
            for m in range(4):
                def one(rr, carry, f=f, m=m):
                    a, b = got[rr * NC + 2 * m, f], got[rr * NC + 2 * m + 1, f]
                    for h in range(2):
                        s = slice(h * 64, h * 64 + 64)
                        to = pl.ds(pl.multiple_of(rr * 32 + h * 16, 16), 16)
                        matrices[f, to, m * 128 : m * 128 + 128] = jnp.concatenate(
                            [a[:, s], b[:, s]], axis=1
                        )
                    return carry

                lax.fori_loop(0, NR, one, 0)
        if outgoing:
            mixed = lax.dot_general(
                matrices[0], matrices[1], (((1,), (1,)), ((), ())), preferred_element_type=F32
            )
        else:
            mixed = lax.dot_general(
                matrices[0], matrices[1], (((0,), (0,)), ((), ())), preferred_element_type=F32
            )
        for rr in range(NR):
            low, high = mixed[rr * 32 : rr * 32 + 16], mixed[rr * 32 + 16 : rr * 32 + 32]
            for m in range(NC):
                s = slice(m * 64, m * 64 + 64)
                back[rr * NC + m] = jnp.concatenate([low[:, s], high[:, s]], axis=1).astype(BF)

    def finish(mixed, weights):
        v = mixed[...].astype(F32)
        spread_l[...] = columns_normed(v).reshape(2048, 128)

        def one(t2, carry):
            sides = []
            for k in range(2):
                sides.append(
                    jnp.concatenate(
                        [spread_l[pl.ds(b * 128 + t2 * 2 + k, 8, stride=16), :] for b in range(16)],
                        axis=0,
                    )
                )
            normed = jnp.concatenate(sides, axis=1).astype(BF)
            at = pl.ds(pl.multiple_of(t2 * 256, 256), 256)
            update = jnp.dot(weights[...], normed, preferred_element_type=F32)
            pair[:, at] += gate[:, at] * update
            return carry

        lax.fori_loop(0, 8, one, 0)

    for n, (weights, final, send, got, back, mixed) in enumerate((
        (out_w, out_f, send1, got1, back1, mix1),
        (in_w, in_f, send2, got2, back2, mix2),
    )):
        project(weights, send)
        exchange(where, send, got, sems.at[2 * n])
        await_exchange(where, send, got, sems.at[2 * n])
        mix(got, back, n == 0)
        exchange(where, back, mixed, sems.at[2 * n + 1])
        await_exchange(where, back, mixed, sems.at[2 * n + 1])
        finish(mixed, final)

    def turn_back(t, carry):
        block = pair[:, pl.ds(pl.multiple_of(t * 128, 128), 128)].T
        result[t] = block[:64]
        result[t + 16] = block[64:]
        return carry

    lax.fori_loop(0, 16, turn_back, 0)


def normalize_layer(values):
    average = jnp.mean(values, axis=-1, keepdims=True)
    centred = values - average
    spread = jnp.mean(centred * centred, axis=-1, keepdims=True)
    return centred * lax.rsqrt(spread + epsilon)


def local(
    alignment,
    pair_state,
    alignment_factor_weight,
    outer_proj,
    outgoing_proj,
    outgoing_final,
    incoming_proj,
    incoming_final,
):
    values = alignment.astype(F32).reshape(16, 64, 64)
    normed = normalize_layer(values).astype(BF)
    factors = jnp.dot(
        normed.reshape(1024, 64), alignment_factor_weight, preferred_element_type=F32
    ).astype(BF).reshape(16, 64, 64)
    row = factors[:, :, :32].reshape(16, 2, 1024).transpose(1, 0, 2)
    col = factors[:, :, 32:].transpose(0, 2, 1).reshape(16, 2048)
    opm_w = outer_proj.reshape(32, 16, 2, 128).transpose(3, 2, 1, 0).reshape(128, 1024)
    vmem = pl.BlockSpec(memory_space=pltpu.VMEM)
    v = pltpu.VMEM
    return pl.pallas_call(
        kernel,
        out_shape=jax.ShapeDtypeStruct((32, 64, 128), F32),
        in_specs=[vmem] * 8,
        out_specs=vmem,
        scratch_shapes=[
            v((256, 2048), BF), v((256, 1024), BF), v((1024, 256), BF), v((1024, 2048), BF),
            v((128, 2048), F32), v((128, 2048), F32), v((2048, 128), F32), v((2048, 128), F32),
            v((2, 512, 512), BF),
            v((128, 2, 16, 128), BF), v((128, 2, 16, 128), BF), v((128, 16, 128), BF), v((128, 16, 128), BF),
            v((128, 2, 16, 128), BF), v((128, 2, 16, 128), BF), v((128, 16, 128), BF), v((128, 16, 128), BF),
            pltpu.SemaphoreType.DMA((4,)),
            pltpu.SemaphoreType.DMA((4, 2)),
        ],
        compiler_params=pltpu.CompilerParams(
            collective_id=0, has_side_effects=True, vmem_limit_bytes=56 << 20
        ),
    )(
        col, row, pair_state, opm_w,
        outgoing_proj.T, outgoing_final.T, incoming_proj.T, incoming_final.T,
    )


def solution(mesh):
    return jax.shard_map(
        local,
        mesh=mesh,
        in_specs=(P("row", "col"), P("row", "col", None), P(), P(), P(), P(), P(), P()),
        out_specs=P("row", "col", None),
        check_vma=False,
    )
```

```python
import functools

import jax
import jax.numpy as jnp
from jax import lax
from jax.experimental import pallas as pl
from jax.experimental.pallas import tpu as pltpu
from jax.sharding import PartitionSpec as P

epsilon = 1e-05
MESH = pl.DeviceIdType.MESH
NR, NC = 16, 8
ND = NR * NC
BF, F32 = jnp.bfloat16, jnp.float32


def sigmoid(x):
    return 0.5 * jnp.tanh(0.5 * x) + 0.5


def position():
    return lax.axis_index("row"), lax.axis_index("col")


def columns_normed(v):
    centred = v - jnp.mean(v, axis=0, keepdims=True)
    spread = jnp.mean(centred * centred, axis=0, keepdims=True)
    return centred * lax.rsqrt(spread + epsilon)


def lanes(at, size):
    return pl.ds(pl.multiple_of(at * size, size), size)


def halves(a, b):
    return (
        jnp.concatenate([a[:, :64], b[:, :64]], axis=1),
        jnp.concatenate([a[:, 64:], b[:, 64:]], axis=1),
    )


def kernel(
    align_ref, factor_ref, pair_ref, opm_ref, out_w, out_f, in_w, in_f, result,
    row_send, col_all, row_all, row_t, outer, pair_in, pair, normed, gate, spread_l, spread_r,
    opm_w, weights, finals, matrices, turned, mixed,
    send1, got1, back1, mix1, send2, got2, back2, mix2, lsem, csems, bsems, sems,
):
    r, c = position()
    me = r * NC + c
    home = (r // 2 == c).astype(jnp.int32)
    bar = pltpu.get_barrier_semaphore()
    load_pair = pltpu.make_async_copy(pair_ref, pair_in, lsem)
    load_pair.start()

    def greet(rr, cc):
        @pl.when(jnp.logical_or(rr != r, cc != c))
        def _():
            pl.semaphore_signal(bar, inc=1, device_id=(rr, cc), device_id_type=MESH)

    def greet_rows(k, carry):
        rr = lax.rem(r + k, NR)
        greet(rr, c)
        greet(rr, r // 2)
        return carry

    def greet_cols(k, carry):
        greet(r, lax.rem(c + k, NC))
        return carry

    lax.fori_loop(0, NR, greet_rows, 0)
    lax.fori_loop(1, NC, greet_cols, 0)

    def by_token(g, carry):
        v = align_ref[:, lanes(g, 128)].astype(F32)
        w = pltpu.roll(v, 64, 1)
        for h in range(2):
            spread_l[pl.ds(h * 512 + 2 * g, 8, stride=64), :] = v[h * 8 : h * 8 + 8]
            spread_l[pl.ds(h * 512 + 2 * g + 1, 8, stride=64), :] = w[h * 8 : h * 8 + 8]
        return carry

    lax.fori_loop(0, 32, by_token, 0, unroll=8)
    values = spread_l[0:1024, 0:64]
    centred = values - jnp.mean(values, axis=-1, keepdims=True)
    spread = jnp.mean(centred * centred, axis=-1, keepdims=True)
    tokens = (centred * lax.rsqrt(spread + epsilon)).astype(BF)
    spread_l[1024:2048, :] = jnp.dot(
        tokens, jnp.concatenate([factor_ref[:, :32]] * 4, axis=1), preferred_element_type=F32
    )
    cols = lax.dot_general(
        factor_ref[...].T, tokens, (((1,), (1,)), ((), ())), preferred_element_type=F32
    )
    for b in range(4):
        for s in range(8):
            spread_r[pl.ds(b * 64 + s, 8, stride=8), :] = cols[
                32 + b * 8 : 40 + b * 8, s * 128 : s * 128 + 128
            ]
    mine = lanes(r, 16)
    for q in range(16):
        a, b = halves(spread_r[q * 16 : q * 16 + 8, :], spread_r[q * 16 + 8 : q * 16 + 16, :])
        col_all[mine, q * 128 : q * 128 + 128] = jnp.concatenate([a, b], axis=0).astype(BF)
    lane = lax.broadcasted_iota(jnp.int32, (16, 128), 1)
    for n in range(16):
        piece = None
        for k in range(4):
            at = 1024 + n * 4 + k
            v = jnp.concatenate(
                [spread_l[pl.ds(at, 8, stride=128), :], spread_l[pl.ds(at + 64, 8, stride=128), :]], axis=0
            )
            piece = v if k == 0 else jnp.where(lane < 32 * k, piece, v)
        row_send[n // 8, :, n % 8 * 128 : n % 8 * 128 + 128] = piece.astype(BF)

    pl.semaphore_wait(bar, (NR - 1) + (NC - 1) + NR - home)

    def send_row(k, carry):
        half, cc = lax.rem(k, 2), lax.rem(c + k // 2, NC)
        rr = 2 * c + half

        @pl.when(jnp.logical_or(rr != r, cc != c))
        def _():
            pltpu.make_async_remote_copy(
                row_send.at[half], row_all.at[mine], bsems.at[0], bsems.at[1],
                device_id=(rr, cc), device_id_type=MESH,
            ).start()

        return carry

    sibling = r + 1 - 2 * lax.rem(r, 2)

    def col_copy(rr, at, send_sem, got_sem):
        block = col_all.at[lanes(at, 16)]
        return pltpu.make_async_remote_copy(
            block, block, send_sem, got_sem, device_id=(rr, c), device_id_type=MESH
        )

    for k in range(1, 8):
        col_copy(lax.rem(r + 2 * k, NR), r, csems.at[0], csems.at[1 + k]).start()
    col_copy(sibling, r, csems.at[9], csems.at[10]).start()
    lax.fori_loop(0, NR, send_row, 0)

    @pl.when(home == 1)
    def _():
        row_all[mine] = row_send[lax.rem(r, 2)]

    for n, (w, f) in enumerate(((out_w, out_f), (in_w, in_f))):
        for b in range(5):
            weights[n, b] = w[:, b * 128 : b * 128 + 128].T
        finals[n] = f[...].T
    spread_l[0:1024, :] = opm_ref[...].astype(F32)
    for q in range(8):
        block = jnp.concatenate(
            [
                spread_l[pl.ds((q % 4 * 4 + k) * 2 + q // 4 + p * 256, 8, stride=32), :]
                for k in range(4)
                for p in range(4)
            ],
            axis=0,
        )
        opm_w[:, q * 128 : q * 128 + 128] = block.T.astype(BF)

    for k in range(1, 8):
        frm = lax.rem(r + 16 - 2 * k, NR)
        col_copy(r, frm, csems.at[0], csems.at[1 + k]).wait_recv()
        col_copy(sibling, frm, csems.at[9], csems.at[10]).start()

    load_pair.wait()

    def turn(t, carry):
        block = jnp.concatenate([pair_in[t], pair_in[t + 16]], axis=0)
        pair[:, lanes(t, 128)] = block.T
        return carry

    lax.fori_loop(0, 16, turn, 0)

    @pl.when(home == 1)
    def _():
        part = row_all.at[pl.ds(0, 15 * 16)]
        pltpu.make_async_remote_copy(
            part, part, bsems.at[0], bsems.at[1], device_id=(r, c), device_id_type=MESH
        ).wait()

    @pl.when(home == 0)
    def _():
        pltpu.make_async_remote_copy(
            row_all, row_all, bsems.at[0], bsems.at[1], device_id=(r, c), device_id_type=MESH
        ).wait()

    row_t[...] = row_all[...].T
    seven, eight = col_all.at[pl.ds(0, 7 * 16)], col_all.at[pl.ds(0, 8 * 16)]
    pltpu.make_async_remote_copy(
        seven, seven, csems.at[0], csems.at[1], device_id=(r, c), device_id_type=MESH
    ).wait_send()
    pltpu.make_async_remote_copy(
        eight, eight, csems.at[9], csems.at[10], device_id=(r, c), device_id_type=MESH
    ).wait()

    def outer_part(n, carry):
        at = lanes(n, 256)
        outer[:, at] = jnp.dot(row_t[...], col_all[:, at], preferred_element_type=F32).astype(BF)
        return carry

    lax.fori_loop(0, 8, outer_part, 0)

    def opm(t2, carry):
        sides = []
        for k in range(2):
            t = t2 * 2 + k
            low = outer[lanes(t, 32), :]
            high = outer[lanes(t + 16, 32), :]
            evens, odds = [], []
            for q in range(16):
                a, b = halves(low[:, q * 128 : q * 128 + 128], high[:, q * 128 : q * 128 + 128])
                evens.append(a)
                odds.append(b)
            sides.append(jnp.concatenate(evens + odds, axis=0))
        term = jnp.dot(opm_w[...], jnp.concatenate(sides, axis=1), preferred_element_type=F32)
        at = lanes(t2, 256)
        now = pair[:, at] + term * (1.0 / 256.0)
        pair[:, at] = now
        normed[:, at] = columns_normed(now).astype(BF)
        return carry

    lax.fori_loop(0, 8, opm, 0)

    def send_group(q, source, target, pairsems):
        def one(k, carry):
            rr, cc = q * 4 + k // NC, lax.rem(c + k, NC)

            @pl.when(jnp.logical_or(rr != r, cc != c))
            def _():
                pltpu.make_async_remote_copy(
                    source.at[rr * NC + cc], target.at[me], pairsems.at[0], pairsems.at[1],
                    device_id=(rr, cc), device_id_type=MESH,
                ).start()

            return carry

        lax.fori_loop(0, 32, one, 0)

    def await_all(source, target, pairsems):
        pltpu.make_async_remote_copy(
            source.at[pl.ds(0, ND - 1)], target.at[pl.ds(0, ND - 1)], pairsems.at[0], pairsems.at[1],
            device_id=(r, c), device_id_type=MESH,
        ).wait()

    def project(n, send, got, pairsems):
        def group(g, carry):
            q = lax.rem(r // 4 + g, 4)
            w = jnp.concatenate([weights[n, b, lanes(q, 32), :] for b in range(4)], axis=0)
            for m in range(4):
                p = jnp.dot(w, normed[:, m * 512 : m * 512 + 512], preferred_element_type=F32)
                left = sigmoid(p[:32]) * p[32:64]
                right = sigmoid(p[64:96]) * p[96:]
                for k in range(4):
                    for b in range(4):
                        to = pl.ds(b * 128 + m * 4 + k, 8, stride=16)
                        spread_l[to, :] = left[b * 8 : b * 8 + 8, k * 128 : k * 128 + 128]
                        spread_r[to, :] = right[b * 8 : b * 8 + 8, k * 128 : k * 128 + 128]
            to = lanes(q, 32)
            send[to, 0] = spread_l[0:512, :].astype(BF).reshape(32, 16, 128)
            send[to, 1] = spread_r[0:512, :].astype(BF).reshape(32, 16, 128)
            send_group(q, send, got, pairsems)
            return carry

        lax.fori_loop(0, 4, group, 0)
        got[me] = send[me]

        def gates(m, carry):
            at = lanes(m, 256)
            gate[:, at] = sigmoid(jnp.dot(weights[n, 4], normed[:, at], preferred_element_type=F32))
            return carry

        lax.fori_loop(0, 8, gates, 0)
        await_all(send, got, pairsems)

    def mix(n, got, back, target, pairsems):
        def place(rr, carry):
            for f in range(2):
                for m in range(4):
                    both = halves(got[rr * NC + 2 * m, f], got[rr * NC + 2 * m + 1, f])
                    for h in range(2):
                        to = pl.ds(pl.multiple_of(rr * 32 + h * 16, 16), 16)
                        matrices[f, to, m * 128 : m * 128 + 128] = both[h]
            return carry

        lax.fori_loop(0, NR, place, 0)
        turned[...] = matrices[1 - n].T

        def group(g, carry):
            q = lax.rem(r // 4 + g, 4)
            at = lanes(q, 128)
            left, right = (matrices[0, at, :], turned[...]) if n == 0 else (turned[at, :], matrices[1])
            mixed[...] = jnp.dot(left, right, preferred_element_type=F32)
            for k in range(4):
                for m in range(4):
                    s = slice(m * 128, m * 128 + 128)
                    both = halves(mixed[k * 32 : k * 32 + 16, s], mixed[k * 32 + 16 : k * 32 + 32, s])
                    for h in range(2):
                        back[(q * 4 + k) * NC + 2 * m + h] = both[h].astype(BF)
            send_group(q, back, target, pairsems)
            return carry

        lax.fori_loop(0, 4, group, 0)
        target[me] = back[me]
        await_all(back, target, pairsems)

    def finish(n, mixed):
        spread_l[...] = mixed[...].astype(F32).reshape(2048, 128)

        def one(t2, carry):
            sides = []
            for k in range(2):
                sides.append(
                    jnp.concatenate(
                        [spread_l[pl.ds(b * 128 + t2 * 2 + k, 8, stride=16), :] for b in range(16)],
                        axis=0,
                    )
                )
            v = columns_normed(jnp.concatenate(sides, axis=1)).astype(BF)
            at = lanes(t2, 256)
            now = pair[:, at] + gate[:, at] * jnp.dot(finals[n], v, preferred_element_type=F32)
            if n == 0:
                pair[:, at] = now
                normed[:, at] = columns_normed(now).astype(BF)
            else:
                for k in range(2):
                    block = now[:, k * 128 : k * 128 + 128].T
                    result[t2 * 2 + k] = block[:64]
                    result[t2 * 2 + k + 16] = block[64:]
            return carry

        lax.fori_loop(0, 8, one, 0)

    for n, (send, got, back, target) in enumerate(
        ((send1, got1, back1, mix1), (send2, got2, back2, mix2))
    ):
        project(n, send, got, sems.at[2 * n])
        mix(n, got, back, target, sems.at[2 * n + 1])
        finish(n, target)


def local(
    alignment,
    pair_state,
    alignment_factor_weight,
    outer_proj,
    outgoing_proj,
    outgoing_final,
    incoming_proj,
    incoming_final,
):
    vmem = pl.BlockSpec(memory_space=pltpu.VMEM)
    anywhere = pl.BlockSpec(memory_space=pl.ANY)
    v = pltpu.VMEM
    exchanged = [
        v((128, 2, 16, 128), BF), v((128, 2, 16, 128), BF), v((128, 16, 128), BF), v((128, 16, 128), BF),
    ]
    return pl.pallas_call(
        kernel,
        out_shape=jax.ShapeDtypeStruct((32, 64, 128), F32),
        in_specs=[vmem, vmem, anywhere] + [vmem] * 5,
        out_specs=vmem,
        scratch_shapes=[
            v((2, 16, 1024), BF), v((256, 2048), BF), v((256, 1024), BF), v((1024, 256), BF),
            v((1024, 2048), BF), v((32, 64, 128), F32), v((128, 2048), F32), v((128, 2048), BF),
            v((128, 2048), F32), v((2048, 128), F32), v((2048, 128), F32),
            v((128, 1024), BF), v((2, 5, 128, 128), BF), v((2, 128, 128), BF),
            v((2, 512, 512), BF), v((512, 512), BF), v((128, 512), F32),
            *exchanged, *exchanged,
            pltpu.SemaphoreType.DMA,
            pltpu.SemaphoreType.DMA((11,)),
            pltpu.SemaphoreType.DMA((2,)),
            pltpu.SemaphoreType.DMA((4, 2)),
        ],
        compiler_params=pltpu.CompilerParams(
            collective_id=0, has_side_effects=True, vmem_limit_bytes=56 << 20
        ),
    )(
        alignment, alignment_factor_weight, pair_state, outer_proj,
        outgoing_proj, outgoing_final, incoming_proj, incoming_final,
    )


def solution(mesh):
    return jax.shard_map(
        local,
        mesh=mesh,
        in_specs=(P("row", "col"), P("row", "col", None), P(), P(), P(), P(), P(), P()),
        out_specs=P("row", "col", None),
        check_vma=False,
    )
```

```python
import functools

import jax
import jax.numpy as jnp
from jax import lax
from jax.experimental import pallas as pl
from jax.experimental.pallas import tpu as pltpu
from jax.sharding import PartitionSpec as P

epsilon = 1e-05
MESH = pl.DeviceIdType.MESH
NR, NC = 16, 8
ND = NR * NC
BF, F32 = jnp.bfloat16, jnp.float32


def sigmoid(x):
    return 0.5 * jnp.tanh(0.5 * x) + 0.5


def position():
    return lax.axis_index("row"), lax.axis_index("col")


def columns_normed(v):
    centred = v - jnp.mean(v, axis=0, keepdims=True)
    spread = jnp.mean(centred * centred, axis=0, keepdims=True)
    return centred * lax.rsqrt(spread + epsilon)


def lanes(at, size):
    return pl.ds(pl.multiple_of(at * size, size), size)


def halves(a, b):
    return (
        jnp.concatenate([a[:, :64], b[:, :64]], axis=1),
        jnp.concatenate([a[:, 64:], b[:, 64:]], axis=1),
    )


def kernel(
    align_hbm, factor_hbm, pair_hbm, opm_hbm, out_w_hbm, out_f_hbm, in_w_hbm, in_f_hbm, result,
    align_ref, factor_ref, pair_in, opm_ref, out_w, out_f, in_w, in_f, row_send, col_all, row_all, row_t, outer, pair, normed, gate, spread_l, spread_r,
    opm_w, weights, finals, matrices, turned, mixed,
    send1, got1, back1, mix1, send2, got2, back2, mix2, lsem, csems, bsems, sems,
):
    r, c = position()
    me = r * NC + c
    z, group_here = r // 2 % 4, r // 8 * 2 + r % 2
    channel = group_here * 32 + z * NC + c
    home = (r // 2 == c).astype(jnp.int32)
    bar = pltpu.get_barrier_semaphore()
    loads = [
        pltpu.make_async_copy(source, to, lsem.at[k])
        for k, (source, to) in enumerate((
            (align_hbm, align_ref), (factor_hbm, factor_ref), (pair_hbm, pair_in), (opm_hbm, opm_ref),
            (out_w_hbm, out_w), (out_f_hbm, out_f), (in_w_hbm, in_w), (in_f_hbm, in_f),
        ))
    ]
    for load in loads:
        load.start()

    def greet(rr, cc):
        @pl.when(jnp.logical_or(rr != r, cc != c))
        def _():
            pl.semaphore_signal(bar, inc=1, device_id=(rr, cc), device_id_type=MESH)

    def greet_rows(k, carry):
        rr = (r + k) & 15
        greet(rr, c)
        greet(rr, r // 2)
        return carry

    def greet_cols(k, carry):
        greet(r, (c + k) & 7)
        return carry

    lax.fori_loop(0, NR, greet_rows, 0)
    lax.fori_loop(1, NC, greet_cols, 0)

    loads[0].wait()
    loads[1].wait()

    def by_token(g, carry):
        v = align_ref[:, lanes(g, 128)].astype(F32)
        w = pltpu.roll(v, 64, 1)
        for h in range(2):
            spread_l[pl.ds(h * 512 + 2 * g, 8, stride=64), :] = v[h * 8 : h * 8 + 8]
            spread_l[pl.ds(h * 512 + 2 * g + 1, 8, stride=64), :] = w[h * 8 : h * 8 + 8]
        return carry

    lax.fori_loop(0, 32, by_token, 0, unroll=8)
    values = spread_l[0:1024, 0:64]
    centred = values - jnp.mean(values, axis=-1, keepdims=True)
    spread = jnp.mean(centred * centred, axis=-1, keepdims=True)
    tokens = (centred * lax.rsqrt(spread + epsilon)).astype(BF)
    spread_l[1024:2048, :] = jnp.dot(
        tokens, jnp.concatenate([factor_ref[:, :32]] * 4, axis=1), preferred_element_type=F32
    )
    cols = lax.dot_general(
        factor_ref[...].T, tokens, (((1,), (1,)), ((), ())), preferred_element_type=F32
    )
    for b in range(4):
        for s in range(8):
            spread_r[pl.ds(b * 64 + s, 8, stride=8), :] = cols[
                32 + b * 8 : 40 + b * 8, s * 128 : s * 128 + 128
            ]
    mine = lanes(r, 16)
    for q in range(16):
        a, b = halves(spread_r[q * 16 : q * 16 + 8, :], spread_r[q * 16 + 8 : q * 16 + 16, :])
        col_all[mine, q * 128 : q * 128 + 128] = jnp.concatenate([a, b], axis=0).astype(BF)
    lane = lax.broadcasted_iota(jnp.int32, (16, 128), 1)
    for n in range(16):
        piece = None
        for k in range(4):
            at = 1024 + n * 4 + k
            v = jnp.concatenate(
                [spread_l[pl.ds(at, 8, stride=128), :], spread_l[pl.ds(at + 64, 8, stride=128), :]], axis=0
            )
            piece = v if k == 0 else jnp.where(lane < 32 * k, piece, v)
        row_send[n // 8, :, n % 8 * 128 : n % 8 * 128 + 128] = piece.astype(BF)

    pl.semaphore_wait(bar, (NR - 1) + (NC - 1) + NR - home)

    def send_row(k, carry):
        half, cc = k & 1, (c + k // 2) & 7
        rr = 2 * c + half

        @pl.when(jnp.logical_or(rr != r, cc != c))
        def _():
            pltpu.make_async_remote_copy(
                row_send.at[half], row_all.at[mine], bsems.at[0], bsems.at[1],
                device_id=(rr, cc), device_id_type=MESH,
            ).start()

        return carry

    sibling = r + 1 - 2 * lax.rem(r, 2)

    def col_copy(rr, at, send_sem, got_sem):
        block = col_all.at[lanes(at, 16)]
        return pltpu.make_async_remote_copy(
            block, block, send_sem, got_sem, device_id=(rr, c), device_id_type=MESH
        )

    for k in range(1, 8):
        col_copy(lax.rem(r + 2 * k, NR), r, csems.at[0], csems.at[1 + k]).start()
    col_copy(sibling, r, csems.at[9], csems.at[10]).start()
    lax.fori_loop(0, NR, send_row, 0)

    @pl.when(home == 1)
    def _():
        row_all[mine] = row_send[lax.rem(r, 2)]

    for load in loads[3:]:
        load.wait()
    for n, (w, f) in enumerate(((out_w, out_f), (in_w, in_f))):
        for b in range(5):
            weights[n, b] = w[:, b * 128 : b * 128 + 128].T
        finals[n] = f[...].T
    spread_l[0:1024, :] = opm_ref[...].astype(F32)
    for q in range(8):
        block = jnp.concatenate(
            [
                spread_l[pl.ds((q % 4 * 4 + k) * 2 + q // 4 + p * 256, 8, stride=32), :]
                for k in range(4)
                for p in range(4)
            ],
            axis=0,
        )
        opm_w[:, q * 128 : q * 128 + 128] = block.T.astype(BF)

    for k in range(1, 8):
        frm = lax.rem(r + 16 - 2 * k, NR)
        col_copy(r, frm, csems.at[0], csems.at[1 + k]).wait_recv()
        col_copy(sibling, frm, csems.at[9], csems.at[10]).start()

    loads[2].wait()

    def turn(t, carry):
        block = jnp.concatenate([pair_in[t], pair_in[t + 16]], axis=0)
        pair[:, lanes(t, 128)] = block.T
        return carry

    lax.fori_loop(0, 16, turn, 0, unroll=8)

    @pl.when(home == 1)
    def _():
        part = row_all.at[pl.ds(0, 15 * 16)]
        pltpu.make_async_remote_copy(
            part, part, bsems.at[0], bsems.at[1], device_id=(r, c), device_id_type=MESH
        ).wait()

    @pl.when(home == 0)
    def _():
        pltpu.make_async_remote_copy(
            row_all, row_all, bsems.at[0], bsems.at[1], device_id=(r, c), device_id_type=MESH
        ).wait()

    row_t[...] = row_all[...].T
    seven, eight = col_all.at[pl.ds(0, 7 * 16)], col_all.at[pl.ds(0, 8 * 16)]
    pltpu.make_async_remote_copy(
        seven, seven, csems.at[0], csems.at[1], device_id=(r, c), device_id_type=MESH
    ).wait_send()
    pltpu.make_async_remote_copy(
        eight, eight, csems.at[9], csems.at[10], device_id=(r, c), device_id_type=MESH
    ).wait()

    def outer_part(n, carry):
        at = lanes(n, 256)
        outer[:, at] = jnp.dot(row_t[...], col_all[:, at], preferred_element_type=F32).astype(BF)
        return carry

    lax.fori_loop(0, 8, outer_part, 0, unroll=4)

    def opm(t2, carry):
        sides = []
        for k in range(2):
            t = t2 * 2 + k
            low = outer[lanes(t, 32), :]
            high = outer[lanes(t + 16, 32), :]
            evens, odds = [], []
            for q in range(16):
                a, b = halves(low[:, q * 128 : q * 128 + 128], high[:, q * 128 : q * 128 + 128])
                evens.append(a)
                odds.append(b)
            sides.append(jnp.concatenate(evens + odds, axis=0))
        term = jnp.dot(opm_w[...], jnp.concatenate(sides, axis=1), preferred_element_type=F32)
        at = lanes(t2, 256)
        now = pair[:, at] + term * (1.0 / 256.0)
        pair[:, at] = now
        normed[:, at] = columns_normed(now).astype(BF)
        return carry

    lax.fori_loop(0, 8, opm, 0, unroll=4)

    def send_group(q, source, target, by_channel, pairsems):
        def one(k, carry):
            zz, cc = (z + k // NC) & 3, (c + k) & 7
            rr = (q // 2) * 8 + zz * 2 + q % 2

            @pl.when(jnp.logical_or(rr != r, cc != c))
            def _():
                pltpu.make_async_remote_copy(
                    source.at[q * 32 + zz * NC + cc if by_channel else rr * NC + cc],
                    target.at[me if by_channel else channel],
                    pairsems.at[0], pairsems.at[1],
                    device_id=(rr, cc), device_id_type=MESH,
                ).start()

            return carry

        lax.fori_loop(0, 32, one, 0)

    def await_all(source, target, pairsems):
        pltpu.make_async_remote_copy(
            source.at[pl.ds(0, ND - 1)], target.at[pl.ds(0, ND - 1)], pairsems.at[0], pairsems.at[1],
            device_id=(r, c), device_id_type=MESH,
        ).wait()

    def project(n, send, got, pairsems):
        def group(g, carry):
            q = (group_here + g) & 3
            w = jnp.concatenate([weights[n, b, lanes(q, 32), :] for b in range(4)], axis=0)
            for m in range(4):
                p = jnp.dot(w, normed[:, m * 512 : m * 512 + 512], preferred_element_type=F32)
                left = sigmoid(p[:32]) * p[32:64]
                right = sigmoid(p[64:96]) * p[96:]
                for k in range(4):
                    for b in range(4):
                        to = pl.ds(b * 128 + m * 4 + k, 8, stride=16)
                        spread_l[to, :] = left[b * 8 : b * 8 + 8, k * 128 : k * 128 + 128]
                        spread_r[to, :] = right[b * 8 : b * 8 + 8, k * 128 : k * 128 + 128]
            to = lanes(q, 32)
            send[to, 0] = spread_l[0:512, :].astype(BF).reshape(32, 16, 128)
            send[to, 1] = spread_r[0:512, :].astype(BF).reshape(32, 16, 128)
            send_group(q, send, got, True, pairsems)
            return carry

        lax.fori_loop(0, 4, group, 0)
        got[me] = send[channel]

        def gates(m, carry):
            at = lanes(m, 256)
            gate[:, at] = sigmoid(jnp.dot(weights[n, 4], normed[:, at], preferred_element_type=F32))
            return carry

        lax.fori_loop(0, 8, gates, 0, unroll=4)
        await_all(send, got, pairsems)

    def mix(n, got, back, target, pairsems):
        def place(rr, carry):
            for f in range(2):
                for m in range(4):
                    both = halves(got[rr * NC + 2 * m, f], got[rr * NC + 2 * m + 1, f])
                    for h in range(2):
                        to = pl.ds(pl.multiple_of(rr * 32 + h * 16, 16), 16)
                        matrices[f, to, m * 128 : m * 128 + 128] = both[h]
            return carry

        lax.fori_loop(0, NR, place, 0, unroll=8)
        turned[...] = matrices[1 - n].T

        def group(g, carry):
            q = (group_here + g) & 3
            first = (q // 2) * 8 + q % 2
            rows, right = (matrices.at[0], turned[...]) if n == 0 else (turned, matrices[1])
            left = jnp.concatenate([rows[lanes(first + 2 * k, 32), :] for k in range(4)], axis=0)
            mixed[...] = jnp.dot(left, right, preferred_element_type=F32)
            for k in range(4):
                for m in range(4):
                    s = slice(m * 128, m * 128 + 128)
                    both = halves(mixed[k * 32 : k * 32 + 16, s], mixed[k * 32 + 16 : k * 32 + 32, s])
                    for h in range(2):
                        back[(first + 2 * k) * NC + 2 * m + h] = both[h].astype(BF)
            send_group(q, back, target, False, pairsems)
            return carry

        lax.fori_loop(0, 4, group, 0)
        target[channel] = back[me]
        await_all(back, target, pairsems)

    def finish(n, mixed):
        spread_l[...] = mixed[...].astype(F32).reshape(2048, 128)

        def one(t2, carry):
            sides = []
            for k in range(2):
                sides.append(
                    jnp.concatenate(
                        [spread_l[pl.ds(b * 128 + t2 * 2 + k, 8, stride=16), :] for b in range(16)],
                        axis=0,
                    )
                )
            v = columns_normed(jnp.concatenate(sides, axis=1)).astype(BF)
            at = lanes(t2, 256)
            now = pair[:, at] + gate[:, at] * jnp.dot(finals[n], v, preferred_element_type=F32)
            if n == 0:
                pair[:, at] = now
                normed[:, at] = columns_normed(now).astype(BF)
            else:
                for k in range(2):
                    block = now[:, k * 128 : k * 128 + 128].T
                    result[t2 * 2 + k] = block[:64]
                    result[t2 * 2 + k + 16] = block[64:]
            return carry

        lax.fori_loop(0, 8, one, 0, unroll=8)

    for n, (send, got, back, target) in enumerate(
        ((send1, got1, back1, mix1), (send2, got2, back2, mix2))
    ):
        project(n, send, got, sems.at[2 * n])
        mix(n, got, back, target, sems.at[2 * n + 1])
        finish(n, target)


def local(
    alignment,
    pair_state,
    alignment_factor_weight,
    outer_proj,
    outgoing_proj,
    outgoing_final,
    incoming_proj,
    incoming_final,
):
    vmem = pl.BlockSpec(memory_space=pltpu.VMEM)
    hbm = pl.BlockSpec(memory_space=pltpu.HBM)
    v = pltpu.VMEM
    exchanged = [
        v((128, 2, 16, 128), BF), v((128, 2, 16, 128), BF), v((128, 16, 128), BF), v((128, 16, 128), BF),
    ]
    return pl.pallas_call(
        kernel,
        out_shape=jax.ShapeDtypeStruct((32, 64, 128), F32),
        in_specs=[hbm] * 8,
        out_specs=vmem,
        scratch_shapes=[
            v((16, 4096), BF), v((64, 64), BF), v((32, 64, 128), F32), v((1024, 128), BF),
            v((128, 640), BF), v((128, 128), BF), v((128, 640), BF), v((128, 128), BF),
            v((2, 16, 1024), BF), v((256, 2048), BF), v((256, 1024), BF), v((1024, 256), BF),
            v((1024, 2048), BF), v((128, 2048), F32), v((128, 2048), BF),
            v((128, 2048), F32), v((2048, 128), F32), v((2048, 128), F32),
            v((128, 1024), BF), v((2, 5, 128, 128), BF), v((2, 128, 128), BF),
            v((2, 512, 512), BF), v((512, 512), BF), v((128, 512), F32),
            *exchanged, *exchanged,
            pltpu.SemaphoreType.DMA((8,)),
            pltpu.SemaphoreType.DMA((11,)),
            pltpu.SemaphoreType.DMA((2,)),
            pltpu.SemaphoreType.DMA((4, 2)),
        ],
        compiler_params=pltpu.CompilerParams(
            collective_id=0, has_side_effects=True, vmem_limit_bytes=56 << 20
        ),
    )(
        alignment, alignment_factor_weight, pair_state, outer_proj,
        outgoing_proj, outgoing_final, incoming_proj, incoming_final,
    )


def solution(mesh):
    return jax.shard_map(
        local,
        mesh=mesh,
        in_specs=(P("row", "col"), P("row", "col", None), P(), P(), P(), P(), P(), P()),
        out_specs=P("row", "col", None),
        check_vma=False,
    )
```

```python
import functools

import jax
import jax.numpy as jnp
from jax import lax
from jax.experimental import pallas as pl
from jax.experimental.pallas import tpu as pltpu
from jax.sharding import PartitionSpec as P

epsilon = 1e-05
MESH = pl.DeviceIdType.MESH
NR, NC = 16, 8
ND = NR * NC
BF, F32 = jnp.bfloat16, jnp.float32


def sigmoid(x):
    return 0.5 * jnp.tanh(0.5 * x) + 0.5


def position():
    return lax.axis_index("row"), lax.axis_index("col")


def columns_normed(v):
    centred = v - jnp.mean(v, axis=0, keepdims=True)
    spread = jnp.mean(centred * centred, axis=0, keepdims=True)
    return centred * lax.rsqrt(spread + epsilon)


def lanes(at, size):
    return pl.ds(pl.multiple_of(at * size, size), size)


def halves(a, b):
    return (
        jnp.concatenate([a[:, :64], b[:, :64]], axis=1),
        jnp.concatenate([a[:, 64:], b[:, 64:]], axis=1),
    )


def kernel(
    align_hbm, factor_hbm, pair_hbm, opm_hbm, out_w_hbm, out_f_hbm, in_w_hbm, in_f_hbm, result,
    align_ref, factor_ref, pair_in, opm_ref, out_w, out_f, in_w, in_f, row_send, col_all, row_all, row_t, outer, pair, normed, gate, spread_l, spread_r,
    opm_w, weights, finals, matrices, turned, mixed,
    send1, got1, back1, mix1, send2, got2, back2, mix2, lsem, csems, bsems, sems,
):
    r, c = position()
    me = r * NC + c
    z, group_here = r // 2 % 4, r // 8 * 2 + r % 2
    channel = group_here * 32 + z * NC + c
    home = (r // 2 == c).astype(jnp.int32)
    bar = pltpu.get_barrier_semaphore()
    loads = [
        pltpu.make_async_copy(source, to, lsem.at[k])
        for k, (source, to) in enumerate((
            (align_hbm, align_ref), (factor_hbm, factor_ref), (pair_hbm, pair_in), (opm_hbm, opm_ref),
            (out_w_hbm, out_w), (out_f_hbm, out_f), (in_w_hbm, in_w), (in_f_hbm, in_f),
        ))
    ]
    for load in loads:
        load.start()

    def greet(rr, cc):
        pl.semaphore_signal(bar, inc=1, device_id=(rr, cc), device_id_type=MESH)

    def beside(k):
        return (r // 8) * 8 + (z + k) % 4 * 2 + r % 2

    sibling, across = r + 1 - 2 * (r % 2), (r + 8) % NR
    for rr in (sibling, across, beside(1), beside(2), beside(3)):
        greet(rr, c)

    def greet_sources(k, carry):
        rr = (r + k) & 15

        @pl.when(jnp.logical_or(k > 0, home == 0))
        def _():
            greet(rr, r // 2)

        return carry

    lax.fori_loop(0, NR, greet_sources, 0)

    loads[0].wait()
    loads[1].wait()

    def by_token(g, carry):
        v = align_ref[:, lanes(g, 128)].astype(F32)
        w = pltpu.roll(v, 64, 1)
        for h in range(2):
            spread_l[pl.ds(h * 512 + 2 * g, 8, stride=64), :] = v[h * 8 : h * 8 + 8]
            spread_l[pl.ds(h * 512 + 2 * g + 1, 8, stride=64), :] = w[h * 8 : h * 8 + 8]
        return carry

    lax.fori_loop(0, 32, by_token, 0, unroll=8)
    values = spread_l[0:1024, 0:64]
    centred = values - jnp.mean(values, axis=-1, keepdims=True)
    spread = jnp.mean(centred * centred, axis=-1, keepdims=True)
    tokens = (centred * lax.rsqrt(spread + epsilon)).astype(BF)
    spread_l[1024:2048, :] = jnp.dot(
        tokens, jnp.concatenate([factor_ref[:, :32]] * 4, axis=1), preferred_element_type=F32
    )
    cols = lax.dot_general(
        factor_ref[...].T, tokens, (((1,), (1,)), ((), ())), preferred_element_type=F32
    )
    for b in range(4):
        for s in range(8):
            spread_r[pl.ds(b * 64 + s, 8, stride=8), :] = cols[
                32 + b * 8 : 40 + b * 8, s * 128 : s * 128 + 128
            ]
    mine = lanes(r, 16)
    for q in range(16):
        a, b = halves(spread_r[q * 16 : q * 16 + 8, :], spread_r[q * 16 + 8 : q * 16 + 16, :])
        col_all[mine, q * 128 : q * 128 + 128] = jnp.concatenate([a, b], axis=0).astype(BF)
    lane = lax.broadcasted_iota(jnp.int32, (16, 128), 1)
    for n in range(16):
        piece = None
        for k in range(4):
            at = 1024 + n * 4 + k
            v = jnp.concatenate(
                [spread_l[pl.ds(at, 8, stride=128), :], spread_l[pl.ds(at + 64, 8, stride=128), :]], axis=0
            )
            piece = v if k == 0 else jnp.where(lane < 32 * k, piece, v)
        row_send[n // 8, n % 8] = piece.astype(BF)

    pl.semaphore_wait(bar, 5 + NR - home)

    def send_row(k, carry):
        half, cc = k & 1, (c + k // 2) & 7
        rr = 2 * c + half

        @pl.when(jnp.logical_or(rr != r, cc != c))
        def _():
            pltpu.make_async_remote_copy(
                row_send.at[half, cc], row_all.at[cc, mine], bsems.at[0], bsems.at[1],
                device_id=(rr, cc), device_id_type=MESH,
            ).start()

        return carry

    lax.fori_loop(0, NR, send_row, 0)

    def col_copy(rr, at, send_sem, got_sem):
        block = col_all.at[lanes(at, 16)]
        return pltpu.make_async_remote_copy(
            block, block, csems.at[send_sem], csems.at[got_sem], device_id=(rr, c), device_id_type=MESH
        )

    col_copy(across, r, 0, 1).start()
    for k in range(1, 4):
        col_copy(beside(k), r, 0, 1 + k).start()
    col_copy(sibling, r, 8, 9).start()

    @pl.when(home == 1)
    def _():
        row_all[c, mine] = row_send[r % 2, c]

    for load in loads[3:]:
        load.wait()
    for n, (w, f) in enumerate(((out_w, out_f), (in_w, in_f))):
        for b in range(5):
            weights[n, b] = w[:, b * 128 : b * 128 + 128].T
        finals[n] = f[...].T
    spread_l[0:1024, :] = opm_ref[...].astype(F32)
    for q in range(8):
        block = jnp.concatenate(
            [
                spread_l[pl.ds((q % 4 * 4 + k) * 2 + q // 4 + p * 256, 8, stride=32), :]
                for k in range(4)
                for p in range(4)
            ],
            axis=0,
        )
        opm_w[:, q * 128 : q * 128 + 128] = block.T.astype(BF)

    col_copy(r, across, 0, 1).wait_recv()
    for k in range(1, 4):
        col_copy(beside(k), across, 0, 4 + k).start()
    col_copy(sibling, across, 8, 9).start()

    def await_rows(part):
        pltpu.make_async_remote_copy(
            part, part, bsems.at[0], bsems.at[1], device_id=(r, c), device_id_type=MESH
        ).wait()

    @pl.when(home == 1)
    def _():
        await_rows(row_all.at[0, pl.ds(0, 15 * 16)])

    @pl.when(home == 0)
    def _():
        await_rows(row_all.at[0])

    for k in range(1, NC):
        part = row_all.at[c]
        pltpu.make_async_remote_copy(
            part, part, bsems.at[2], bsems.at[3], device_id=(r, (c + k) % NC), device_id_type=MESH
        ).start()

    loads[2].wait()

    def turn(t, carry):
        block = jnp.concatenate([pair_in[t], pair_in[t + 16]], axis=0)
        pair[:, lanes(t, 128)] = block.T
        return carry

    lax.fori_loop(0, 16, turn, 0, unroll=8)

    for k in range(1, 4):
        col_copy(r, beside(4 - k), 0, 1 + k).wait_recv()
        col_copy(sibling, beside(4 - k), 8, 9).start()
    for k in range(1, 4):
        col_copy(r, beside(4 - k), 0, 4 + k).wait_recv()
        col_copy(sibling, (beside(4 - k) + 8) % NR, 8, 9).start()
    others = row_all.at[pl.ds(0, NC - 1)]
    pltpu.make_async_remote_copy(
        others, others, bsems.at[2], bsems.at[3], device_id=(r, c), device_id_type=MESH
    ).wait()
    for k in range(NC):
        row_t[k * 128 : k * 128 + 128, :] = row_all[k].T
    seven, eight = col_all.at[pl.ds(0, 7 * 16)], col_all.at[pl.ds(0, 8 * 16)]
    pltpu.make_async_remote_copy(
        seven, seven, csems.at[0], csems.at[1], device_id=(r, c), device_id_type=MESH
    ).wait_send()
    pltpu.make_async_remote_copy(
        eight, eight, csems.at[8], csems.at[9], device_id=(r, c), device_id_type=MESH
    ).wait()

    def outer_part(n, carry):
        at = lanes(n, 256)
        outer[:, at] = jnp.dot(row_t[...], col_all[:, at], preferred_element_type=F32).astype(BF)
        return carry

    lax.fori_loop(0, 8, outer_part, 0, unroll=4)

    def opm(t2, carry):
        sides = []
        for k in range(2):
            t = t2 * 2 + k
            low = outer[lanes(t, 32), :]
            high = outer[lanes(t + 16, 32), :]
            evens, odds = [], []
            for q in range(16):
                a, b = halves(low[:, q * 128 : q * 128 + 128], high[:, q * 128 : q * 128 + 128])
                evens.append(a)
                odds.append(b)
            sides.append(jnp.concatenate(evens + odds, axis=0))
        term = jnp.dot(opm_w[...], jnp.concatenate(sides, axis=1), preferred_element_type=F32)
        at = lanes(t2, 256)
        now = pair[:, at] + term * (1.0 / 256.0)
        pair[:, at] = now
        normed[:, at] = columns_normed(now).astype(BF)
        return carry

    lax.fori_loop(0, 8, opm, 0, unroll=4)

    def row_of(q, zz):
        return (q // 2) * 8 + zz * 2 + q % 2

    def send_one(g, zz, cc, rr, source, target, phases):
        pltpu.make_async_remote_copy(
            source, target, phases.at[0], phases.at[1 + g], device_id=(rr, cc), device_id_type=MESH
        ).start()

    def await_phase(g, got, phases):
        part = got.at[pl.ds(0, 31 if g == 0 else 32)]
        pltpu.make_async_remote_copy(
            part, part, phases.at[0], phases.at[1 + g], device_id=(r, c), device_id_type=MESH
        ).wait_recv()

    def await_sends(source, phases):
        part = source.at[pl.ds(0, ND - 1)]
        pltpu.make_async_remote_copy(
            part, part, phases.at[0], phases.at[1], device_id=(r, c), device_id_type=MESH
        ).wait_send()

    def in_groups(group):
        group(0)

        def later(g, carry):
            group(g)
            return carry

        lax.fori_loop(1, 4, later, 0)

    def project(n, send, got, phases):
        def group(g):
            q = (group_here + g) & 3
            w = jnp.concatenate([weights[n, b, lanes(q, 32), :] for b in range(4)], axis=0)
            for m in range(4):
                p = jnp.dot(w, normed[:, m * 512 : m * 512 + 512], preferred_element_type=F32)
                left = sigmoid(p[:32]) * p[32:64]
                right = sigmoid(p[64:96]) * p[96:]
                for k in range(4):
                    for b in range(4):
                        to = pl.ds(b * 128 + m * 4 + k, 8, stride=16)
                        spread_l[to, :] = left[b * 8 : b * 8 + 8, k * 128 : k * 128 + 128]
                        spread_r[to, :] = right[b * 8 : b * 8 + 8, k * 128 : k * 128 + 128]
            to = lanes(q, 32)
            send[to, 0] = spread_l[0:512, :].astype(BF).reshape(32, 16, 128)
            send[to, 1] = spread_r[0:512, :].astype(BF).reshape(32, 16, 128)

            def one(k, carry):
                zz, cc = (z + k // NC) & 3, (c + k) & 7
                send_one(g, zz, cc, row_of(q, zz), send.at[q * 32 + zz * NC + cc], got.at[me], phases)
                return carry

            lax.fori_loop(1 if isinstance(g, int) else 0, 32, one, 0, unroll=1)

        in_groups(group)
        got[me] = send[channel]

        def gates(m, carry):
            at = lanes(m, 256)
            gate[:, at] = sigmoid(jnp.dot(weights[n, 4], normed[:, at], preferred_element_type=F32))
            return carry

        lax.fori_loop(0, 8, gates, 0, unroll=4)

    def mix(n, send, got, before, back, target, phases):
        for g in range(4):
            source = (group_here - g) & 3
            await_phase(g, got, before)
            for zz in range(4):
                rr = row_of(source, zz)
                grouped = source * 128 + zz * 32
                for f in range(2):
                    start = rr * 32 if n == 0 and f == 1 else grouped
                    for m in range(4):
                        both = halves(got[rr * NC + 2 * m, f], got[rr * NC + 2 * m + 1, f])
                        for h in range(2):
                            to = pl.ds(pl.multiple_of(start + h * 16, 16), 16)
                            matrices[f, to, m * 128 : m * 128 + 128] = both[h]
            if n == 1:
                turned[:, lanes(source, 128)] = matrices[0, lanes(source, 128), :].T
        await_sends(send, before)

        def group(g):
            q = (group_here + g) & 3
            if n == 0:
                rows = [matrices[0, lanes(q * 4 + ((z + k) & 3), 32), :] for k in range(4)]
            else:
                rows = [turned[lanes(row_of(q, (z + k) & 3), 32), :] for k in range(4)]
            left = jnp.concatenate(rows, axis=0)
            if n == 0:
                product = lax.dot_general(
                    left, matrices[1], (((1,), (1,)), ((), ())), preferred_element_type=F32
                )
            else:
                product = jnp.dot(left, matrices[1], preferred_element_type=F32)
            for k in range(4):
                zz = (z + k) & 3
                rr = row_of(q, zz)
                for m in range(4):
                    s = slice(m * 128, m * 128 + 128)
                    both = halves(product[k * 32 : k * 32 + 16, s], product[k * 32 + 16 : k * 32 + 32, s])
                    for h in range(2):
                        back[rr * NC + 2 * m + h] = both[h].astype(BF)
                for i in range(NC):
                    if k == 0 and i == 0 and isinstance(g, int):
                        continue
                    cc = (c + i) & 7
                    send_one(g, zz, cc, rr, back.at[rr * NC + cc], target.at[channel], phases)

        in_groups(group)
        target[channel] = back[me]

    def finish(n, back, mixed, before):
        for g in range(4):
            source = (group_here - g) & 3
            await_phase(g, mixed, before)
            spread_l[lanes(source, 512), :] = mixed[lanes(source, 32)].astype(F32).reshape(512, 128)
        await_sends(back, before)

        def one(t2, carry):
            sides = []
            for k in range(2):
                sides.append(
                    jnp.concatenate(
                        [spread_l[pl.ds(b * 128 + t2 * 2 + k, 8, stride=16), :] for b in range(16)],
                        axis=0,
                    )
                )
            v = columns_normed(jnp.concatenate(sides, axis=1)).astype(BF)
            at = lanes(t2, 256)
            now = pair[:, at] + gate[:, at] * jnp.dot(finals[n], v, preferred_element_type=F32)
            if n == 0:
                pair[:, at] = now
                normed[:, at] = columns_normed(now).astype(BF)
            else:
                for k in range(2):
                    block = now[:, k * 128 : k * 128 + 128].T
                    pair_in[t2 * 2 + k] = block[:64]
                    pair_in[t2 * 2 + k + 16] = block[64:]
                for h in range(2):
                    part = pl.ds(t2 * 2 + h * 16, 2)
                    pltpu.make_async_copy(pair_in.at[part], result.at[part], lsem.at[0]).start()
            return carry

        lax.fori_loop(0, 8, one, 0, unroll=8)
        if n == 1:
            pltpu.make_async_copy(pair_in, result, lsem.at[0]).wait()

    for n, (send, got, back, target) in enumerate(
        ((send1, got1, back1, mix1), (send2, got2, back2, mix2))
    ):
        project(n, send, got, sems.at[2 * n])
        mix(n, send, got, sems.at[2 * n], back, target, sems.at[2 * n + 1])
        finish(n, back, target, sems.at[2 * n + 1])


def local(
    alignment,
    pair_state,
    alignment_factor_weight,
    outer_proj,
    outgoing_proj,
    outgoing_final,
    incoming_proj,
    incoming_final,
):
    vmem = pl.BlockSpec(memory_space=pltpu.VMEM)
    hbm = pl.BlockSpec(memory_space=pltpu.HBM)
    v = pltpu.VMEM
    exchanged = [
        v((128, 2, 16, 128), BF), v((128, 2, 16, 128), BF), v((128, 16, 128), BF), v((128, 16, 128), BF),
    ]
    return pl.pallas_call(
        kernel,
        out_shape=jax.ShapeDtypeStruct((32, 64, 128), F32),
        in_specs=[hbm] * 8,
        out_specs=hbm,
        scratch_shapes=[
            v((16, 4096), BF), v((64, 64), BF), v((32, 64, 128), F32), v((1024, 128), BF),
            v((128, 640), BF), v((128, 128), BF), v((128, 640), BF), v((128, 128), BF),
            v((2, 8, 16, 128), BF), v((256, 2048), BF), v((8, 256, 128), BF), v((1024, 256), BF),
            v((1024, 2048), BF), v((128, 2048), F32), v((128, 2048), BF),
            v((128, 2048), F32), v((2048, 128), F32), v((2048, 128), F32),
            v((128, 1024), BF), v((2, 5, 128, 128), BF), v((2, 128, 128), BF),
            v((2, 512, 512), BF), v((512, 512), BF), v((128, 512), F32),
            *exchanged, *exchanged,
            pltpu.SemaphoreType.DMA((8,)),
            pltpu.SemaphoreType.DMA((10,)),
            pltpu.SemaphoreType.DMA((4,)),
            pltpu.SemaphoreType.DMA((4, 5)),
        ],
        compiler_params=pltpu.CompilerParams(
            collective_id=0, has_side_effects=True, vmem_limit_bytes=56 << 20
        ),
    )(
        alignment, alignment_factor_weight, pair_state, outer_proj,
        outgoing_proj, outgoing_final, incoming_proj, incoming_final,
    )


def solution(mesh):
    return jax.shard_map(
        local,
        mesh=mesh,
        in_specs=(P("row", "col"), P("row", "col", None), P(), P(), P(), P(), P(), P()),
        out_specs=P("row", "col", None),
        check_vma=False,
    )
```

```python
import functools

import jax
import jax.numpy as jnp
from jax import lax
from jax.experimental import pallas as pl
from jax.experimental.pallas import tpu as pltpu
from jax.sharding import PartitionSpec as P

epsilon = 1e-05
MESH = pl.DeviceIdType.MESH
NR, NC = 16, 8
ND = NR * NC
BF, F32 = jnp.bfloat16, jnp.float32


def sigmoid(x):
    return 0.5 * jnp.tanh(0.5 * x) + 0.5


def position():
    return lax.axis_index("row"), lax.axis_index("col")


def columns_normed(v):
    centred = v - jnp.mean(v, axis=0, keepdims=True)
    spread = jnp.mean(centred * centred, axis=0, keepdims=True)
    return centred * lax.rsqrt(spread + epsilon)


def lanes(at, size):
    return pl.ds(pl.multiple_of(at * size, size), size)


def halves(a, b):
    return (
        jnp.concatenate([a[:, :64], b[:, :64]], axis=1),
        jnp.concatenate([a[:, 64:], b[:, 64:]], axis=1),
    )


def kernel(
    align_hbm, factor_hbm, pair_hbm, opm_hbm, out_w_hbm, out_f_hbm, in_w_hbm, in_f_hbm, result,
    align_ref, factor_ref, pair_in, opm_ref, out_w, out_f, in_w, in_f, row_send, col_all, row_all, row_t, outer, pair, normed, gate, spread_l, spread_r,
    opm_w, weights, finals, matrices, turned, mixed,
    send1, got1, back1, mix1, send2, got2, back2, mix2, lsem, csems, bsems, rsems, sems,
):
    r, c = position()
    me = r * NC + c
    z, group_here = r // 2 % 4, r // 8 * 2 + r % 2
    channel = group_here * 32 + z * NC + c
    home = (r // 2 == c).astype(jnp.int32)
    bar = pltpu.get_barrier_semaphore()
    loads = [
        pltpu.make_async_copy(source, to, lsem.at[k])
        for k, (source, to) in enumerate((
            (align_hbm, align_ref), (factor_hbm, factor_ref), (pair_hbm, pair_in), (opm_hbm, opm_ref),
            (out_w_hbm, out_w), (out_f_hbm, out_f), (in_w_hbm, in_w), (in_f_hbm, in_f),
        ))
    ]
    for load in loads:
        load.start()

    def greet(rr, cc):
        pl.semaphore_signal(bar, inc=1, device_id=(rr, cc), device_id_type=MESH)

    def beside(k):
        return (r // 8) * 8 + (z + k) % 4 * 2 + r % 2

    sibling, across = r + 1 - 2 * (r % 2), (r + 8) % NR
    for rr in (sibling, across, beside(1), beside(2), beside(3)):
        greet(rr, c)

    def greet_sources(k, carry):
        rr = (r + k) & 15

        @pl.when(jnp.logical_or(k > 0, home == 0))
        def _():
            greet(rr, r // 2)

        return carry

    lax.fori_loop(0, NR, greet_sources, 0)

    loads[0].wait()
    loads[1].wait()

    def by_token(g, carry):
        v = align_ref[:, lanes(g, 128)].astype(F32)
        w = pltpu.roll(v, 64, 1)
        for h in range(2):
            spread_l[pl.ds(h * 512 + 2 * g, 8, stride=64), :] = v[h * 8 : h * 8 + 8]
            spread_l[pl.ds(h * 512 + 2 * g + 1, 8, stride=64), :] = w[h * 8 : h * 8 + 8]
        return carry

    lax.fori_loop(0, 32, by_token, 0, unroll=8)
    values = spread_l[0:1024, 0:64]
    centred = values - jnp.mean(values, axis=-1, keepdims=True)
    spread = jnp.mean(centred * centred, axis=-1, keepdims=True)
    tokens = (centred * lax.rsqrt(spread + epsilon)).astype(BF)
    spread_l[1024:2048, :] = jnp.dot(
        tokens, jnp.concatenate([factor_ref[:, :32]] * 4, axis=1), preferred_element_type=F32
    )
    cols = lax.dot_general(
        factor_ref[...].T, tokens, (((1,), (1,)), ((), ())), preferred_element_type=F32
    )
    for b in range(4):
        for s in range(8):
            spread_r[pl.ds(b * 64 + s, 8, stride=8), :] = cols[
                32 + b * 8 : 40 + b * 8, s * 128 : s * 128 + 128
            ]
    mine = lanes(r, 16)
    for q in range(16):
        a, b = halves(spread_r[q * 16 : q * 16 + 8, :], spread_r[q * 16 + 8 : q * 16 + 16, :])
        col_all[mine, q * 128 : q * 128 + 128] = jnp.concatenate([a, b], axis=0).astype(BF)
    lane = lax.broadcasted_iota(jnp.int32, (16, 128), 1)
    for n in range(16):
        piece = None
        for k in range(4):
            at = 1024 + n * 4 + k
            v = jnp.concatenate(
                [spread_l[pl.ds(at, 8, stride=128), :], spread_l[pl.ds(at + 64, 8, stride=128), :]], axis=0
            )
            piece = v if k == 0 else jnp.where(lane < 32 * k, piece, v)
        row_send[n // 8, n % 8] = piece.astype(BF)

    pl.semaphore_wait(bar, 5 + NR - home)

    def send_row(k, carry):
        half, cc = k & 1, (c + k // 2) & 7
        rr = 2 * c + half

        @pl.when(jnp.logical_or(rr != r, cc != c))
        def _():
            pltpu.make_async_remote_copy(
                row_send.at[half, cc], row_all.at[cc, mine], bsems.at[0], bsems.at[1],
                device_id=(rr, cc), device_id_type=MESH,
            ).start()

        return carry

    lax.fori_loop(0, NR, send_row, 0)

    def col_copy(rr, at, send_sem, got_sem):
        block = col_all.at[lanes(at, 16)]
        return pltpu.make_async_remote_copy(
            block, block, csems.at[send_sem], csems.at[got_sem], device_id=(rr, c), device_id_type=MESH
        )

    col_copy(across, r, 0, 1).start()
    for k in range(1, 4):
        col_copy(beside(k), r, 0, 1 + k).start()
    col_copy(sibling, r, 8, 9).start()

    @pl.when(home == 1)
    def _():
        row_all[c, mine] = row_send[r % 2, c]

    for load in loads[3:]:
        load.wait()
    for n, (w, f) in enumerate(((out_w, out_f), (in_w, in_f))):
        for b in range(5):
            weights[n, b] = w[:, b * 128 : b * 128 + 128].T
        finals[n] = f[...].T
    spread_l[0:1024, :] = opm_ref[...].astype(F32)
    for q in range(8):
        block = jnp.concatenate(
            [
                spread_l[pl.ds((q % 4 * 4 + k) * 2 + q // 4 + p * 256, 8, stride=32), :]
                for k in range(4)
                for p in range(4)
            ],
            axis=0,
        )
        opm_w[:, q * 128 : q * 128 + 128] = block.T.astype(BF)

    col_copy(r, across, 0, 1).wait_recv()
    for k in range(1, 4):
        col_copy(beside(k), across, 0, 4 + k).start()
    col_copy(sibling, across, 8, 9).start()

    def await_rows(part):
        pltpu.make_async_remote_copy(
            part, part, bsems.at[0], bsems.at[1], device_id=(r, c), device_id_type=MESH
        ).wait()

    @pl.when(home == 1)
    def _():
        await_rows(row_all.at[0, pl.ds(0, 15 * 16)])

    @pl.when(home == 0)
    def _():
        await_rows(row_all.at[0])

    over = c + 1 - 2 * (c % 2)

    def aside(k):
        return (c + 2 * k) % NC

    def row_copy(cc, half, at, send_sem, got_sem):
        part = row_all.at[at, pl.ds(half * 128, 128)]
        return pltpu.make_async_remote_copy(
            part, part, rsems.at[send_sem], rsems.at[got_sem], device_id=(r, cc), device_id_type=MESH
        )

    row_copy(over, 0, c, 0, 2).start()
    for k in range(1, 4):
        row_copy(aside(k), 1, c, 1, 3 + k).start()
    for k in range(1, 4):
        row_copy(aside(k), 0, c, 0, 3).start()
    row_copy(over, 1, c, 1, 7).start()

    loads[2].wait()

    def turn(t, carry):
        block = jnp.concatenate([pair_in[t], pair_in[t + 16]], axis=0)
        pair[:, lanes(t, 128)] = block.T
        return carry

    lax.fori_loop(0, 16, turn, 0, unroll=8)

    row_copy(c, 0, over, 0, 2).wait_recv()
    for k in range(1, 4):
        row_copy(aside(k), 0, over, 0, 3).start()
    for k in range(1, 4):
        row_copy(c, 1, aside(4 - k), 1, 3 + k).wait_recv()
        row_copy(over, 1, aside(4 - k), 1, 7).start()
    for k in range(1, 4):
        col_copy(r, beside(4 - k), 0, 1 + k).wait_recv()
        col_copy(sibling, beside(4 - k), 8, 9).start()
    for k in range(1, 4):
        col_copy(r, beside(4 - k), 0, 4 + k).wait_recv()
        col_copy(sibling, (beside(4 - k) + 8) % NR, 8, 9).start()
    def row_blocks(count, send_sem, got_sem):
        part = row_all.at[pl.ds(0, count), pl.ds(0, 128)]
        return pltpu.make_async_remote_copy(
            part, part, rsems.at[send_sem], rsems.at[got_sem], device_id=(r, c), device_id_type=MESH
        )

    row_blocks(6, 0, 3).wait_recv()
    row_blocks(4, 1, 7).wait_recv()
    row_blocks(7, 0, 3).wait_send()
    row_blocks(7, 1, 7).wait_send()
    for k in range(NC):
        row_t[k * 128 : k * 128 + 128, :] = row_all[k].T
    seven, eight = col_all.at[pl.ds(0, 7 * 16)], col_all.at[pl.ds(0, 8 * 16)]
    pltpu.make_async_remote_copy(
        seven, seven, csems.at[0], csems.at[1], device_id=(r, c), device_id_type=MESH
    ).wait_send()
    pltpu.make_async_remote_copy(
        eight, eight, csems.at[8], csems.at[9], device_id=(r, c), device_id_type=MESH
    ).wait()

    for k in range(4):
        at = slice(k * 256, k * 256 + 256)
        outer[at, :] = jnp.dot(row_t[at, :], col_all[...], preferred_element_type=F32).astype(BF)

    def opm(t2, carry):
        sides = []
        for k in range(2):
            t = t2 * 2 + k
            low = outer[lanes(t, 32), :]
            high = outer[lanes(t + 16, 32), :]
            evens, odds = [], []
            for q in range(16):
                a, b = halves(low[:, q * 128 : q * 128 + 128], high[:, q * 128 : q * 128 + 128])
                evens.append(a)
                odds.append(b)
            sides.append(jnp.concatenate(evens + odds, axis=0))
        term = jnp.dot(opm_w[...], jnp.concatenate(sides, axis=1), preferred_element_type=F32)
        at = lanes(t2, 256)
        now = pair[:, at] + term * (1.0 / 256.0)
        pair[:, at] = now
        normed[:, at] = columns_normed(now).astype(BF)
        return carry

    lax.fori_loop(0, 8, opm, 0, unroll=4)

    def row_of(q, zz):
        return (q // 2) * 8 + zz * 2 + q % 2

    def send_one(g, zz, cc, rr, source, target, phases):
        pltpu.make_async_remote_copy(
            source, target, phases.at[0], phases.at[1 + g], device_id=(rr, cc), device_id_type=MESH
        ).start()

    def await_phase(g, got, phases):
        part = got.at[pl.ds(0, 31 if g == 0 else 32)]
        pltpu.make_async_remote_copy(
            part, part, phases.at[0], phases.at[1 + g], device_id=(r, c), device_id_type=MESH
        ).wait_recv()

    def await_sends(source, phases):
        part = source.at[pl.ds(0, ND - 1)]
        pltpu.make_async_remote_copy(
            part, part, phases.at[0], phases.at[1], device_id=(r, c), device_id_type=MESH
        ).wait_send()

    def in_groups(group):
        group(0)

        def later(g, carry):
            group(g)
            return carry

        lax.fori_loop(1, 4, later, 0)

    def project(n, send, got, phases):
        def group(g):
            q = (group_here + g) & 3
            w = jnp.concatenate([weights[n, b, lanes(q, 32), :] for b in range(4)], axis=0)
            for m in range(4):
                p = jnp.dot(w, normed[:, m * 512 : m * 512 + 512], preferred_element_type=F32)
                left = sigmoid(p[:32]) * p[32:64]
                right = sigmoid(p[64:96]) * p[96:]
                for k in range(4):
                    for b in range(4):
                        to = pl.ds(b * 128 + m * 4 + k, 8, stride=16)
                        spread_l[to, :] = left[b * 8 : b * 8 + 8, k * 128 : k * 128 + 128]
                        spread_r[to, :] = right[b * 8 : b * 8 + 8, k * 128 : k * 128 + 128]
            to = lanes(q, 32)
            send[to, 0] = spread_l[0:512, :].astype(BF).reshape(32, 16, 128)
            send[to, 1] = spread_r[0:512, :].astype(BF).reshape(32, 16, 128)

            def one(k, carry):
                zz, cc = (z + k // NC) & 3, (c + k) & 7
                send_one(g, zz, cc, row_of(q, zz), send.at[q * 32 + zz * NC + cc], got.at[me], phases)
                return carry

            lax.fori_loop(1 if isinstance(g, int) else 0, 32, one, 0, unroll=1)

        in_groups(group)
        got[me] = send[channel]

        def gates(m, carry):
            at = lanes(m, 256)
            gate[:, at] = sigmoid(jnp.dot(weights[n, 4], normed[:, at], preferred_element_type=F32))
            return carry

        lax.fori_loop(0, 8, gates, 0, unroll=4)

    def mix(n, send, got, before, back, target, phases):
        for g in range(4):
            source = (group_here - g) & 3
            await_phase(g, got, before)
            for zz in range(4):
                rr = row_of(source, zz)
                grouped = source * 128 + zz * 32
                for f in range(2):
                    start = rr * 32 if n == 0 and f == 1 else grouped
                    for m in range(4):
                        both = halves(got[rr * NC + 2 * m, f], got[rr * NC + 2 * m + 1, f])
                        for h in range(2):
                            to = pl.ds(pl.multiple_of(start + h * 16, 16), 16)
                            matrices[f, to, m * 128 : m * 128 + 128] = both[h]
            if n == 1:
                turned[:, lanes(source, 128)] = matrices[0, lanes(source, 128), :].T
        await_sends(send, before)

        def group(g):
            q = (group_here + g) & 3
            if n == 0:
                rows = [matrices[0, lanes(q * 4 + ((z + k) & 3), 32), :] for k in range(4)]
            else:
                rows = [turned[lanes(row_of(q, (z + k) & 3), 32), :] for k in range(4)]
            left = jnp.concatenate(rows, axis=0)
            if n == 0:
                product = lax.dot_general(
                    left, matrices[1], (((1,), (1,)), ((), ())), preferred_element_type=F32
                )
            else:
                product = jnp.dot(left, matrices[1], preferred_element_type=F32)
            for k in range(4):
                zz = (z + k) & 3
                rr = row_of(q, zz)
                for m in range(4):
                    s = slice(m * 128, m * 128 + 128)
                    both = halves(product[k * 32 : k * 32 + 16, s], product[k * 32 + 16 : k * 32 + 32, s])
                    for h in range(2):
                        back[rr * NC + 2 * m + h] = both[h].astype(BF)
                for i in range(NC):
                    if k == 0 and i == 0 and isinstance(g, int):
                        continue
                    cc = (c + i) & 7
                    send_one(g, zz, cc, rr, back.at[rr * NC + cc], target.at[channel], phases)

        in_groups(group)
        target[channel] = back[me]

    def finish(n, back, mixed, before):
        for g in range(4):
            source = (group_here - g) & 3
            await_phase(g, mixed, before)
            spread_l[lanes(source, 512), :] = mixed[lanes(source, 32)].astype(F32).reshape(512, 128)
        await_sends(back, before)

        def one(t2, carry):
            sides = []
            for k in range(2):
                sides.append(
                    jnp.concatenate(
                        [spread_l[pl.ds(b * 128 + t2 * 2 + k, 8, stride=16), :] for b in range(16)],
                        axis=0,
                    )
                )
            v = columns_normed(jnp.concatenate(sides, axis=1)).astype(BF)
            at = lanes(t2, 256)
            now = pair[:, at] + gate[:, at] * jnp.dot(finals[n], v, preferred_element_type=F32)
            if n == 0:
                pair[:, at] = now
                normed[:, at] = columns_normed(now).astype(BF)
            else:
                for k in range(2):
                    block = now[:, k * 128 : k * 128 + 128].T
                    pair_in[t2 * 2 + k] = block[:64]
                    pair_in[t2 * 2 + k + 16] = block[64:]
                for h in range(2):
                    part = pl.ds(t2 * 2 + h * 16, 2)
                    pltpu.make_async_copy(pair_in.at[part], result.at[part], lsem.at[0]).start()
            return carry

        lax.fori_loop(0, 8, one, 0, unroll=8)
        if n == 1:
            pltpu.make_async_copy(pair_in, result, lsem.at[0]).wait()

    for n, (send, got, back, target) in enumerate(
        ((send1, got1, back1, mix1), (send2, got2, back2, mix2))
    ):
        project(n, send, got, sems.at[2 * n])
        mix(n, send, got, sems.at[2 * n], back, target, sems.at[2 * n + 1])
        finish(n, back, target, sems.at[2 * n + 1])


def local(
    alignment,
    pair_state,
    alignment_factor_weight,
    outer_proj,
    outgoing_proj,
    outgoing_final,
    incoming_proj,
    incoming_final,
):
    vmem = pl.BlockSpec(memory_space=pltpu.VMEM)
    hbm = pl.BlockSpec(memory_space=pltpu.HBM)
    v = pltpu.VMEM
    exchanged = [
        v((128, 2, 16, 128), BF), v((128, 2, 16, 128), BF), v((128, 16, 128), BF), v((128, 16, 128), BF),
    ]
    return pl.pallas_call(
        kernel,
        out_shape=jax.ShapeDtypeStruct((32, 64, 128), F32),
        in_specs=[hbm] * 8,
        out_specs=hbm,
        scratch_shapes=[
            v((16, 4096), BF), v((64, 64), BF), v((32, 64, 128), F32), v((1024, 128), BF),
            v((128, 640), BF), v((128, 128), BF), v((128, 640), BF), v((128, 128), BF),
            v((2, 8, 16, 128), BF), v((256, 2048), BF), v((8, 256, 128), BF), v((1024, 256), BF),
            v((1024, 2048), BF), v((128, 2048), F32), v((128, 2048), BF),
            v((128, 2048), F32), v((2048, 128), F32), v((2048, 128), F32),
            v((128, 1024), BF), v((2, 5, 128, 128), BF), v((2, 128, 128), BF),
            v((2, 512, 512), BF), v((512, 512), BF), v((128, 512), F32),
            *exchanged, *exchanged,
            pltpu.SemaphoreType.DMA((8,)),
            pltpu.SemaphoreType.DMA((10,)),
            pltpu.SemaphoreType.DMA((2,)),
            pltpu.SemaphoreType.DMA((8,)),
            pltpu.SemaphoreType.DMA((4, 5)),
        ],
        compiler_params=pltpu.CompilerParams(
            collective_id=0, has_side_effects=True, vmem_limit_bytes=56 << 20
        ),
    )(
        alignment, alignment_factor_weight, pair_state, outer_proj,
        outgoing_proj, outgoing_final, incoming_proj, incoming_final,
    )


def solution(mesh):
    return jax.shard_map(
        local,
        mesh=mesh,
        in_specs=(P("row", "col"), P("row", "col", None), P(), P(), P(), P(), P(), P()),
        out_specs=P("row", "col", None),
        check_vma=False,
    )
```

```python
import functools

import jax
import jax.numpy as jnp
from jax import lax
from jax.experimental import pallas as pl
from jax.experimental.pallas import tpu as pltpu
from jax.sharding import PartitionSpec as P

epsilon = 1e-05
MESH = pl.DeviceIdType.MESH
NR, NC = 16, 8
ND = NR * NC
BF, F32 = jnp.bfloat16, jnp.float32


def sigmoid(x):
    return 0.5 * jnp.tanh(0.5 * x) + 0.5


def position():
    return lax.axis_index("row"), lax.axis_index("col")


def columns_normed(v):
    centred = v - jnp.mean(v, axis=0, keepdims=True)
    spread = jnp.mean(centred * centred, axis=0, keepdims=True)
    return centred * lax.rsqrt(spread + epsilon)


def lanes(at, size):
    return pl.ds(pl.multiple_of(at * size, size), size)


def halves(a, b):
    return (
        jnp.concatenate([a[:, :64], b[:, :64]], axis=1),
        jnp.concatenate([a[:, 64:], b[:, 64:]], axis=1),
    )


def kernel(
    align_hbm, factor_hbm, pair_hbm, opm_hbm, out_w_hbm, out_f_hbm, in_w_hbm, in_f_hbm, result,
    align_ref, factor_ref, pair_in, opm_ref, out_w, out_f, in_w, in_f, row_send, col_all, row_all, row_t, outer, pair, normed, gate, spread_l, spread_r,
    opm_w, weights, finals, matrices, turned, mixed,
    send1, got1, back1, mix1, send2, got2, back2, mix2, lsem, csems, bsems, rsems, sems,
):
    r, c = position()
    me = r * NC + c
    z, group_here = r // 2 % 4, r // 8 * 2 + r % 2
    channel = group_here * 32 + z * NC + c
    home = (r // 2 == c).astype(jnp.int32)
    bar = pltpu.get_barrier_semaphore()
    loads = [
        pltpu.make_async_copy(source, to, lsem.at[k])
        for k, (source, to) in enumerate((
            (align_hbm, align_ref), (factor_hbm, factor_ref), (pair_hbm, pair_in), (opm_hbm, opm_ref),
            (out_w_hbm, out_w), (out_f_hbm, out_f), (in_w_hbm, in_w), (in_f_hbm, in_f),
        ))
    ]
    for load in loads:
        load.start()

    def greet(rr, cc):
        pl.semaphore_signal(bar, inc=1, device_id=(rr, cc), device_id_type=MESH)

    def beside(k):
        return (r // 8) * 8 + (z + k) % 4 * 2 + r % 2

    sibling, across = r + 1 - 2 * (r % 2), (r + 8) % NR
    for rr in (sibling, across, beside(1), beside(2), beside(3)):
        greet(rr, c)

    def greet_sources(k, carry):
        rr = (r + k) & 15

        @pl.when(jnp.logical_or(k > 0, home == 0))
        def _():
            greet(rr, r // 2)

        return carry

    lax.fori_loop(0, NR, greet_sources, 0)

    loads[0].wait()
    loads[1].wait()

    def by_token(g, carry):
        v = align_ref[:, lanes(g, 128)].astype(F32)
        w = pltpu.roll(v, 64, 1)
        for h in range(2):
            spread_l[pl.ds(h * 512 + 2 * g, 8, stride=64), :] = v[h * 8 : h * 8 + 8]
            spread_l[pl.ds(h * 512 + 2 * g + 1, 8, stride=64), :] = w[h * 8 : h * 8 + 8]
        return carry

    lax.fori_loop(0, 32, by_token, 0, unroll=8)
    values = spread_l[0:1024, 0:64]
    centred = values - jnp.mean(values, axis=-1, keepdims=True)
    spread = jnp.mean(centred * centred, axis=-1, keepdims=True)
    tokens = (centred * lax.rsqrt(spread + epsilon)).astype(BF)
    spread_l[1024:2048, :] = jnp.dot(
        tokens, jnp.concatenate([factor_ref[:, :32]] * 4, axis=1), preferred_element_type=F32
    )
    cols = lax.dot_general(
        factor_ref[...].T, tokens, (((1,), (1,)), ((), ())), preferred_element_type=F32
    )
    for b in range(4):
        for s in range(8):
            spread_r[pl.ds(b * 64 + s, 8, stride=8), :] = cols[
                32 + b * 8 : 40 + b * 8, s * 128 : s * 128 + 128
            ]
    mine = lanes(r, 16)
    for q in range(16):
        a, b = halves(spread_r[q * 16 : q * 16 + 8, :], spread_r[q * 16 + 8 : q * 16 + 16, :])
        col_all[mine, q * 128 : q * 128 + 128] = jnp.concatenate([a, b], axis=0).astype(BF)
    lane = lax.broadcasted_iota(jnp.int32, (16, 128), 1)
    for n in range(16):
        piece = None
        for k in range(4):
            at = 1024 + n * 4 + k
            v = jnp.concatenate(
                [spread_l[pl.ds(at, 8, stride=128), :], spread_l[pl.ds(at + 64, 8, stride=128), :]], axis=0
            )
            piece = v if k == 0 else jnp.where(lane < 32 * k, piece, v)
        row_send[n // 8, n % 8] = piece.astype(BF)

    pl.semaphore_wait(bar, 5 + NR - home)

    def send_row(k, carry):
        half, cc = k & 1, (c + k // 2) & 7
        rr = 2 * c + half

        @pl.when(jnp.logical_or(rr != r, cc != c))
        def _():
            pltpu.make_async_remote_copy(
                row_send.at[half, cc], row_all.at[cc, mine], bsems.at[0], bsems.at[1],
                device_id=(rr, cc), device_id_type=MESH,
            ).start()

        return carry

    lax.fori_loop(0, NR, send_row, 0)

    def col_copy(rr, at, send_sem, got_sem):
        block = col_all.at[lanes(at, 16)]
        return pltpu.make_async_remote_copy(
            block, block, csems.at[send_sem], csems.at[got_sem], device_id=(rr, c), device_id_type=MESH
        )

    col_copy(across, r, 0, 1).start()
    for k in range(1, 4):
        col_copy(beside(k), r, 0, 1 + k).start()
    col_copy(sibling, r, 8, 9).start()

    @pl.when(home == 1)
    def _():
        row_all[c, mine] = row_send[r % 2, c]

    for load in loads[3:]:
        load.wait()
    for n, (w, f) in enumerate(((out_w, out_f), (in_w, in_f))):
        for b in range(5):
            weights[n, b] = w[:, b * 128 : b * 128 + 128].T
        finals[n] = f[...].T
    spread_l[0:1024, :] = opm_ref[...].astype(F32)
    for q in range(8):
        block = jnp.concatenate(
            [
                spread_l[pl.ds((q % 4 * 4 + k) * 2 + q // 4 + p * 256, 8, stride=32), :]
                for k in range(4)
                for p in range(4)
            ],
            axis=0,
        )
        opm_w[:, q * 128 : q * 128 + 128] = block.T.astype(BF)

    col_copy(r, across, 0, 1).wait_recv()
    for k in range(1, 4):
        col_copy(beside(k), across, 0, 4 + k).start()
    col_copy(sibling, across, 8, 9).start()

    def await_rows(part):
        pltpu.make_async_remote_copy(
            part, part, bsems.at[0], bsems.at[1], device_id=(r, c), device_id_type=MESH
        ).wait()

    @pl.when(home == 1)
    def _():
        await_rows(row_all.at[0, pl.ds(0, 15 * 16)])

    @pl.when(home == 0)
    def _():
        await_rows(row_all.at[0])

    over = c + 1 - 2 * (c % 2)

    def aside(k):
        return (c + 2 * k) % NC

    def row_copy(cc, half, at, send_sem, got_sem):
        part = row_all.at[at, pl.ds(half * 128, 128)]
        return pltpu.make_async_remote_copy(
            part, part, rsems.at[send_sem], rsems.at[got_sem], device_id=(r, cc), device_id_type=MESH
        )

    row_copy(over, 0, c, 0, 2).start()
    for k in range(1, 4):
        row_copy(aside(k), 1, c, 1, 3 + k).start()
    for k in range(1, 4):
        row_copy(aside(k), 0, c, 0, 3).start()
    row_copy(over, 1, c, 1, 7).start()

    loads[2].wait()

    def turn(t, carry):
        block = jnp.concatenate([pair_in[t], pair_in[t + 16]], axis=0)
        pair[:, lanes(t, 128)] = block.T
        return carry

    lax.fori_loop(0, 16, turn, 0, unroll=8)

    row_copy(c, 0, over, 0, 2).wait_recv()
    for k in range(1, 4):
        row_copy(aside(k), 0, over, 0, 3).start()
    for k in range(1, 4):
        row_copy(c, 1, aside(4 - k), 1, 3 + k).wait_recv()
        row_copy(over, 1, aside(4 - k), 1, 7).start()
    for k in range(1, 4):
        col_copy(r, beside(4 - k), 0, 1 + k).wait_recv()
        col_copy(sibling, beside(4 - k), 8, 9).start()
    for k in range(1, 4):
        col_copy(r, beside(4 - k), 0, 4 + k).wait_recv()
        col_copy(sibling, (beside(4 - k) + 8) % NR, 8, 9).start()
    def row_blocks(count, send_sem, got_sem):
        part = row_all.at[pl.ds(0, count), pl.ds(0, 128)]
        return pltpu.make_async_remote_copy(
            part, part, rsems.at[send_sem], rsems.at[got_sem], device_id=(r, c), device_id_type=MESH
        )

    row_blocks(6, 0, 3).wait_recv()
    row_blocks(4, 1, 7).wait_recv()
    row_blocks(7, 0, 3).wait_send()
    row_blocks(7, 1, 7).wait_send()
    for k in range(NC):
        row_t[k * 128 : k * 128 + 128, :] = row_all[k].T
    seven, eight = col_all.at[pl.ds(0, 7 * 16)], col_all.at[pl.ds(0, 8 * 16)]
    pltpu.make_async_remote_copy(
        seven, seven, csems.at[0], csems.at[1], device_id=(r, c), device_id_type=MESH
    ).wait_send()
    pltpu.make_async_remote_copy(
        eight, eight, csems.at[8], csems.at[9], device_id=(r, c), device_id_type=MESH
    ).wait()

    for k in range(4):
        at = slice(k * 256, k * 256 + 256)
        outer[at, :] = jnp.dot(row_t[at, :], col_all[...], preferred_element_type=F32).astype(BF)

    def opm(t2, carry):
        sides = []
        for k in range(2):
            t = t2 * 2 + k
            low = outer[lanes(t, 32), :]
            high = outer[lanes(t + 16, 32), :]
            evens, odds = [], []
            for q in range(16):
                a, b = halves(low[:, q * 128 : q * 128 + 128], high[:, q * 128 : q * 128 + 128])
                evens.append(a)
                odds.append(b)
            sides.append(jnp.concatenate(evens + odds, axis=0))
        term = jnp.dot(opm_w[...], jnp.concatenate(sides, axis=1), preferred_element_type=F32)
        at = lanes(t2, 256)
        now = pair[:, at] + term * (1.0 / 256.0)
        pair[:, at] = now
        normed[:, at] = columns_normed(now).astype(BF)
        return carry

    lax.fori_loop(0, 8, opm, 0, unroll=8)

    def row_of(q, zz):
        return (q // 2) * 8 + zz * 2 + q % 2

    def send_one(g, zz, cc, rr, source, target, phases):
        pltpu.make_async_remote_copy(
            source, target, phases.at[0], phases.at[1 + g], device_id=(rr, cc), device_id_type=MESH
        ).start()

    def await_phase(g, got, phases):
        part = got.at[pl.ds(0, 31 if g == 0 else 32)]
        pltpu.make_async_remote_copy(
            part, part, phases.at[0], phases.at[1 + g], device_id=(r, c), device_id_type=MESH
        ).wait_recv()

    def await_sends(source, phases):
        part = source.at[pl.ds(0, ND - 1)]
        pltpu.make_async_remote_copy(
            part, part, phases.at[0], phases.at[1], device_id=(r, c), device_id_type=MESH
        ).wait_send()

    def in_groups(group):
        group(0)

        def later(g, carry):
            group(g)
            return carry

        lax.fori_loop(1, 4, later, 0)

    def project(n, send, got, phases):
        def group(g):
            q = (group_here + g) & 3
            w = jnp.concatenate([weights[n, b, lanes(q, 32), :] for b in range(4)], axis=0)
            for m in range(4):
                p = jnp.dot(w, normed[:, m * 512 : m * 512 + 512], preferred_element_type=F32)
                left = sigmoid(p[:32]) * p[32:64]
                right = sigmoid(p[64:96]) * p[96:]
                for k in range(4):
                    for b in range(4):
                        to = pl.ds(b * 128 + m * 4 + k, 8, stride=16)
                        spread_l[to, :] = left[b * 8 : b * 8 + 8, k * 128 : k * 128 + 128]
                        spread_r[to, :] = right[b * 8 : b * 8 + 8, k * 128 : k * 128 + 128]
            to = lanes(q, 32)
            send[to, 0] = spread_l[0:512, :].astype(BF).reshape(32, 16, 128)
            send[to, 1] = spread_r[0:512, :].astype(BF).reshape(32, 16, 128)

            def one(k, carry):
                zz, cc = (z + k // NC) & 3, (c + k) & 7
                send_one(g, zz, cc, row_of(q, zz), send.at[q * 32 + zz * NC + cc], got.at[me], phases)
                return carry

            lax.fori_loop(1 if isinstance(g, int) else 0, 32, one, 0, unroll=1)

        in_groups(group)
        got[me] = send[channel]

        def gates(m, carry):
            at = lanes(m, 256)
            gate[:, at] = sigmoid(jnp.dot(weights[n, 4], normed[:, at], preferred_element_type=F32))
            return carry

        lax.fori_loop(0, 8, gates, 0, unroll=4)

    def mix(n, send, got, before, back, target, phases):
        for g in range(4):
            source = (group_here - g) & 3
            await_phase(g, got, before)
            for zz in range(4):
                rr = row_of(source, zz)
                grouped = source * 128 + zz * 32
                for f in range(2):
                    start = rr * 32 if n == 0 and f == 1 else grouped
                    for m in range(4):
                        both = halves(got[rr * NC + 2 * m, f], got[rr * NC + 2 * m + 1, f])
                        for h in range(2):
                            to = pl.ds(pl.multiple_of(start + h * 16, 16), 16)
                            matrices[f, to, m * 128 : m * 128 + 128] = both[h]
            if n == 1:
                turned[:, lanes(source, 128)] = matrices[0, lanes(source, 128), :].T
        await_sends(send, before)

        def group(g):
            q = (group_here + g) & 3
            if n == 0:
                rows = [matrices[0, lanes(q * 4 + ((z + k) & 3), 32), :] for k in range(4)]
            else:
                rows = [turned[lanes(row_of(q, (z + k) & 3), 32), :] for k in range(4)]
            left = jnp.concatenate(rows, axis=0)
            if n == 0:
                product = lax.dot_general(
                    left, matrices[1], (((1,), (1,)), ((), ())), preferred_element_type=F32
                )
            else:
                product = jnp.dot(left, matrices[1], preferred_element_type=F32)
            for k in range(4):
                zz = (z + k) & 3
                rr = row_of(q, zz)
                for m in range(4):
                    s = slice(m * 128, m * 128 + 128)
                    both = halves(product[k * 32 : k * 32 + 16, s], product[k * 32 + 16 : k * 32 + 32, s])
                    for h in range(2):
                        back[rr * NC + 2 * m + h] = both[h].astype(BF)
                for i in range(NC):
                    if k == 0 and i == 0 and isinstance(g, int):
                        continue
                    cc = (c + i) & 7
                    send_one(g, zz, cc, rr, back.at[rr * NC + cc], target.at[channel], phases)

        in_groups(group)
        target[channel] = back[me]

    def finish(n, back, mixed, before):
        for g in range(4):
            source = (group_here - g) & 3
            await_phase(g, mixed, before)
            spread_l[lanes(source, 512), :] = mixed[lanes(source, 32)].astype(F32).reshape(512, 128)
        await_sends(back, before)

        def one(t2, carry):
            sides = []
            for k in range(2):
                sides.append(
                    jnp.concatenate(
                        [spread_l[pl.ds(b * 128 + t2 * 2 + k, 8, stride=16), :] for b in range(16)],
                        axis=0,
                    )
                )
            v = columns_normed(jnp.concatenate(sides, axis=1)).astype(BF)
            at = lanes(t2, 256)
            now = pair[:, at] + gate[:, at] * jnp.dot(finals[n], v, preferred_element_type=F32)
            if n == 0:
                pair[:, at] = now
                normed[:, at] = columns_normed(now).astype(BF)
            else:
                for k in range(2):
                    block = now[:, k * 128 : k * 128 + 128].T
                    pair_in[t2 * 2 + k] = block[:64]
                    pair_in[t2 * 2 + k + 16] = block[64:]
                for h in range(2):
                    part = pl.ds(t2 * 2 + h * 16, 2)
                    pltpu.make_async_copy(pair_in.at[part], result.at[part], lsem.at[0]).start()
            return carry

        lax.fori_loop(0, 8, one, 0, unroll=8)
        if n == 1:
            pltpu.make_async_copy(pair_in, result, lsem.at[0]).wait()

    for n, (send, got, back, target) in enumerate(
        ((send1, got1, back1, mix1), (send2, got2, back2, mix2))
    ):
        project(n, send, got, sems.at[2 * n])
        mix(n, send, got, sems.at[2 * n], back, target, sems.at[2 * n + 1])
        finish(n, back, target, sems.at[2 * n + 1])


def local(
    alignment,
    pair_state,
    alignment_factor_weight,
    outer_proj,
    outgoing_proj,
    outgoing_final,
    incoming_proj,
    incoming_final,
):
    vmem = pl.BlockSpec(memory_space=pltpu.VMEM)
    hbm = pl.BlockSpec(memory_space=pltpu.HBM)
    v = pltpu.VMEM
    exchanged = [
        v((128, 2, 16, 128), BF), v((128, 2, 16, 128), BF), v((128, 16, 128), BF), v((128, 16, 128), BF),
    ]
    return pl.pallas_call(
        kernel,
        out_shape=jax.ShapeDtypeStruct((32, 64, 128), F32),
        in_specs=[hbm] * 8,
        out_specs=hbm,
        scratch_shapes=[
            v((16, 4096), BF), v((64, 64), BF), v((32, 64, 128), F32), v((1024, 128), BF),
            v((128, 640), BF), v((128, 128), BF), v((128, 640), BF), v((128, 128), BF),
            v((2, 8, 16, 128), BF), v((256, 2048), BF), v((8, 256, 128), BF), v((1024, 256), BF),
            v((1024, 2048), BF), v((128, 2048), F32), v((128, 2048), BF),
            v((128, 2048), F32), v((2048, 128), F32), v((2048, 128), F32),
            v((128, 1024), BF), v((2, 5, 128, 128), BF), v((2, 128, 128), BF),
            v((2, 512, 512), BF), v((512, 512), BF), v((128, 512), F32),
            *exchanged, *exchanged,
            pltpu.SemaphoreType.DMA((8,)),
            pltpu.SemaphoreType.DMA((10,)),
            pltpu.SemaphoreType.DMA((2,)),
            pltpu.SemaphoreType.DMA((8,)),
            pltpu.SemaphoreType.DMA((4, 5)),
        ],
        compiler_params=pltpu.CompilerParams(
            collective_id=0, has_side_effects=True, vmem_limit_bytes=56 << 20
        ),
    )(
        alignment, alignment_factor_weight, pair_state, outer_proj,
        outgoing_proj, outgoing_final, incoming_proj, incoming_final,
    )


def solution(mesh):
    return jax.shard_map(
        local,
        mesh=mesh,
        in_specs=(P("row", "col"), P("row", "col", None), P(), P(), P(), P(), P(), P()),
        out_specs=P("row", "col", None),
        check_vma=False,
    )
```

```python
import functools

import jax
import jax.numpy as jnp
from jax import lax
from jax.experimental import pallas as pl
from jax.experimental.pallas import tpu as pltpu
from jax.sharding import PartitionSpec as P

epsilon = 1e-05
MESH = pl.DeviceIdType.MESH
NR, NC = 16, 8
ND = NR * NC
BF, F32 = jnp.bfloat16, jnp.float32


def sigmoid(x):
    return 0.5 * jnp.tanh(0.5 * x) + 0.5


def position():
    return lax.axis_index("row"), lax.axis_index("col")


def columns_normed(v):
    centred = v - jnp.mean(v, axis=0, keepdims=True)
    spread = jnp.mean(centred * centred, axis=0, keepdims=True)
    return centred * lax.rsqrt(spread + epsilon)


def lanes(at, size):
    return pl.ds(pl.multiple_of(at * size, size), size)


def halves(a, b):
    return (
        jnp.concatenate([a[:, :64], b[:, :64]], axis=1),
        jnp.concatenate([a[:, 64:], b[:, 64:]], axis=1),
    )


def kernel(
    align_hbm, factor_hbm, pair_hbm, opm_hbm, out_w_hbm, out_f_hbm, in_w_hbm, in_f_hbm, result,
    align_ref, factor_ref, pair_in, opm_ref, out_w, out_f, in_w, in_f, row_send, col_all, row_all, row_t, outer, pair, normed, gate, spread_l, spread_r,
    opm_w, weights, finals, matrices, turned, mixed,
    send1, got1, back1, mix1, send2, got2, back2, mix2, lsem, csems, bsems, rsems, sems,
):
    r, c = position()
    me = r * NC + c
    z, group_here = r // 2 % 4, r // 8 * 2 + r % 2
    channel = group_here * 32 + z * NC + c
    home = (r // 2 == c).astype(jnp.int32)
    bar = pltpu.get_barrier_semaphore()
    loads = [
        pltpu.make_async_copy(source, to, lsem.at[k])
        for k, (source, to) in enumerate((
            (align_hbm, align_ref), (factor_hbm, factor_ref), (pair_hbm, pair_in), (opm_hbm, opm_ref),
            (out_w_hbm, out_w), (out_f_hbm, out_f), (in_w_hbm, in_w), (in_f_hbm, in_f),
        ))
    ]
    for load in loads:
        load.start()

    def greet(rr, cc):
        pl.semaphore_signal(bar, inc=1, device_id=(rr, cc), device_id_type=MESH)

    def beside(k):
        return (r // 8) * 8 + (z + k) % 4 * 2 + r % 2

    sibling, across = r + 1 - 2 * (r % 2), (r + 8) % NR
    for rr in (sibling, across, beside(1), beside(2), beside(3)):
        greet(rr, c)

    def greet_sources(k, carry):
        rr = (r + k) & 15

        @pl.when(jnp.logical_or(k > 0, home == 0))
        def _():
            greet(rr, r // 2)

        return carry

    lax.fori_loop(0, NR, greet_sources, 0)

    loads[0].wait()
    loads[1].wait()

    def by_token(g, carry):
        v = align_ref[:, lanes(g, 128)].astype(F32)
        w = pltpu.roll(v, 64, 1)
        for h in range(2):
            spread_l[pl.ds(h * 512 + 2 * g, 8, stride=64), :] = v[h * 8 : h * 8 + 8]
            spread_l[pl.ds(h * 512 + 2 * g + 1, 8, stride=64), :] = w[h * 8 : h * 8 + 8]
        return carry

    lax.fori_loop(0, 32, by_token, 0, unroll=8)
    values = spread_l[0:1024, 0:64]
    centred = values - jnp.mean(values, axis=-1, keepdims=True)
    spread = jnp.mean(centred * centred, axis=-1, keepdims=True)
    tokens = (centred * lax.rsqrt(spread + epsilon)).astype(BF)
    spread_l[1024:2048, :] = jnp.dot(
        tokens, jnp.concatenate([factor_ref[:, :32]] * 4, axis=1), preferred_element_type=F32
    )
    cols = lax.dot_general(
        factor_ref[...].T, tokens, (((1,), (1,)), ((), ())), preferred_element_type=F32
    )
    for b in range(4):
        for s in range(8):
            spread_r[pl.ds(b * 64 + s, 8, stride=8), :] = cols[
                32 + b * 8 : 40 + b * 8, s * 128 : s * 128 + 128
            ]
    mine = lanes(r, 16)
    for q in range(16):
        a, b = halves(spread_r[q * 16 : q * 16 + 8, :], spread_r[q * 16 + 8 : q * 16 + 16, :])
        col_all[mine, q * 128 : q * 128 + 128] = jnp.concatenate([a, b], axis=0).astype(BF)
    lane = lax.broadcasted_iota(jnp.int32, (16, 128), 1)
    for n in range(16):
        piece = None
        for k in range(4):
            at = 1024 + n * 4 + k
            v = jnp.concatenate(
                [spread_l[pl.ds(at, 8, stride=128), :], spread_l[pl.ds(at + 64, 8, stride=128), :]], axis=0
            )
            piece = v if k == 0 else jnp.where(lane < 32 * k, piece, v)
        row_send[n // 8, n % 8] = piece.astype(BF)

    pl.semaphore_wait(bar, 5 + NR - home)

    def send_row(k, carry):
        half, cc = k & 1, (c + k // 2) & 7
        rr = 2 * c + half

        @pl.when(jnp.logical_or(rr != r, cc != c))
        def _():
            pltpu.make_async_remote_copy(
                row_send.at[half, cc], row_all.at[cc, mine], bsems.at[0], bsems.at[1],
                device_id=(rr, cc), device_id_type=MESH,
            ).start()

        return carry

    lax.fori_loop(0, NR, send_row, 0)

    def col_copy(rr, at, send_sem, got_sem):
        block = col_all.at[lanes(at, 16)]
        return pltpu.make_async_remote_copy(
            block, block, csems.at[send_sem], csems.at[got_sem], device_id=(rr, c), device_id_type=MESH
        )

    col_copy(across, r, 0, 1).start()
    for k in range(1, 4):
        col_copy(beside(k), r, 0, 1 + k).start()
    col_copy(sibling, r, 8, 9).start()

    @pl.when(home == 1)
    def _():
        row_all[c, mine] = row_send[r % 2, c]

    for load in loads[3:]:
        load.wait()
    for n, (w, f) in enumerate(((out_w, out_f), (in_w, in_f))):
        for b in range(5):
            weights[n, b] = w[:, b * 128 : b * 128 + 128].T
        finals[n] = f[...].T
    spread_l[0:1024, :] = opm_ref[...].astype(F32)
    for q in range(8):
        block = jnp.concatenate(
            [
                spread_l[pl.ds((q % 4 * 4 + k) * 2 + q // 4 + p * 256, 8, stride=32), :]
                for k in range(4)
                for p in range(4)
            ],
            axis=0,
        )
        opm_w[:, q * 128 : q * 128 + 128] = block.T.astype(BF)

    col_copy(r, across, 0, 1).wait_recv()
    for k in range(1, 4):
        col_copy(beside(k), across, 0, 4 + k).start()
    col_copy(sibling, across, 8, 9).start()

    def await_rows(part):
        pltpu.make_async_remote_copy(
            part, part, bsems.at[0], bsems.at[1], device_id=(r, c), device_id_type=MESH
        ).wait()

    @pl.when(home == 1)
    def _():
        await_rows(row_all.at[0, pl.ds(0, 15 * 16)])

    @pl.when(home == 0)
    def _():
        await_rows(row_all.at[0])

    over = c + 1 - 2 * (c % 2)

    def aside(k):
        return (c + 2 * k) % NC

    def row_copy(cc, half, at, send_sem, got_sem):
        part = row_all.at[at, pl.ds(half * 128, 128)]
        return pltpu.make_async_remote_copy(
            part, part, rsems.at[send_sem], rsems.at[got_sem], device_id=(r, cc), device_id_type=MESH
        )

    row_copy(over, 0, c, 0, 2).start()
    for k in range(1, 4):
        row_copy(aside(k), 1, c, 1, 3 + k).start()
    for k in range(1, 4):
        row_copy(aside(k), 0, c, 0, 3).start()
    row_copy(over, 1, c, 1, 7).start()

    loads[2].wait()

    def turn(t, carry):
        block = jnp.concatenate([pair_in[t], pair_in[t + 16]], axis=0)
        pair[:, lanes(t, 128)] = block.T
        return carry

    lax.fori_loop(0, 16, turn, 0, unroll=8)

    row_copy(c, 0, over, 0, 2).wait_recv()
    for k in range(1, 4):
        row_copy(aside(k), 0, over, 0, 3).start()
    for k in range(1, 4):
        row_copy(c, 1, aside(4 - k), 1, 3 + k).wait_recv()
        row_copy(over, 1, aside(4 - k), 1, 7).start()
    for k in range(1, 4):
        col_copy(r, beside(4 - k), 0, 1 + k).wait_recv()
        col_copy(sibling, beside(4 - k), 8, 9).start()
    for k in range(1, 4):
        col_copy(r, beside(4 - k), 0, 4 + k).wait_recv()
        col_copy(sibling, (beside(4 - k) + 8) % NR, 8, 9).start()
    def row_blocks(count, send_sem, got_sem):
        part = row_all.at[pl.ds(0, count), pl.ds(0, 128)]
        return pltpu.make_async_remote_copy(
            part, part, rsems.at[send_sem], rsems.at[got_sem], device_id=(r, c), device_id_type=MESH
        )

    row_blocks(6, 0, 3).wait_recv()
    row_blocks(4, 1, 7).wait_recv()
    row_blocks(7, 0, 3).wait_send()
    row_blocks(7, 1, 7).wait_send()
    for k in range(NC):
        row_t[k * 128 : k * 128 + 128, :] = row_all[k].T
    seven, eight = col_all.at[pl.ds(0, 7 * 16)], col_all.at[pl.ds(0, 8 * 16)]
    pltpu.make_async_remote_copy(
        seven, seven, csems.at[0], csems.at[1], device_id=(r, c), device_id_type=MESH
    ).wait_send()
    pltpu.make_async_remote_copy(
        eight, eight, csems.at[8], csems.at[9], device_id=(r, c), device_id_type=MESH
    ).wait()

    for k in range(4):
        at = slice(k * 256, k * 256 + 256)
        outer[at, :] = jnp.dot(row_t[at, :], col_all[...], preferred_element_type=F32).astype(BF)

    def opm(t2, carry):
        sides = []
        for k in range(2):
            t = t2 * 2 + k
            low = outer[lanes(t, 32), :]
            high = outer[lanes(t + 16, 32), :]
            evens, odds = [], []
            for q in range(16):
                a, b = halves(low[:, q * 128 : q * 128 + 128], high[:, q * 128 : q * 128 + 128])
                evens.append(a)
                odds.append(b)
            sides.append(jnp.concatenate(evens + odds, axis=0))
        term = jnp.dot(opm_w[...], jnp.concatenate(sides, axis=1), preferred_element_type=F32)
        at = lanes(t2, 256)
        now = pair[:, at] + term * (1.0 / 256.0)
        pair[:, at] = now
        normed[:, at] = columns_normed(now).astype(BF)
        return carry

    lax.fori_loop(0, 8, opm, 0, unroll=8)

    def row_of(q, zz):
        return (q // 2) * 8 + zz * 2 + q % 2

    def send_one(g, zz, cc, rr, source, target, phases):
        pltpu.make_async_remote_copy(
            source, target, phases.at[0], phases.at[1 + g], device_id=(rr, cc), device_id_type=MESH
        ).start()

    def await_phase(g, got, phases):
        part = got.at[pl.ds(0, 31 if g == 0 else 32)]
        pltpu.make_async_remote_copy(
            part, part, phases.at[0], phases.at[1 + g], device_id=(r, c), device_id_type=MESH
        ).wait_recv()

    def await_sends(source, phases):
        part = source.at[pl.ds(0, ND - 1)]
        pltpu.make_async_remote_copy(
            part, part, phases.at[0], phases.at[1], device_id=(r, c), device_id_type=MESH
        ).wait_send()

    def in_groups(group):
        group(0)

        def later(g, carry):
            group(g)
            return carry

        lax.fori_loop(1, 4, later, 0)

    def project(n, send, got, phases):
        def group(g):
            q = (group_here + g) & 3
            w = jnp.concatenate([weights[n, b, lanes(q, 32), :] for b in range(4)], axis=0)
            for m in range(4):
                p = jnp.dot(w, normed[:, m * 512 : m * 512 + 512], preferred_element_type=F32)
                left = sigmoid(p[:32]) * p[32:64]
                right = sigmoid(p[64:96]) * p[96:]
                for k in range(4):
                    for b in range(4):
                        to = pl.ds(b * 128 + m * 4 + k, 8, stride=16)
                        spread_l[to, :] = left[b * 8 : b * 8 + 8, k * 128 : k * 128 + 128]
                        spread_r[to, :] = right[b * 8 : b * 8 + 8, k * 128 : k * 128 + 128]
            to = lanes(q, 32)
            send[to, 0] = spread_l[0:512, :].astype(BF).reshape(32, 16, 128)
            send[to, 1] = spread_r[0:512, :].astype(BF).reshape(32, 16, 128)

            def one(k, carry):
                zz, cc = (z + k // NC) & 3, (c + k) & 7
                send_one(g, zz, cc, row_of(q, zz), send.at[q * 32 + zz * NC + cc], got.at[me], phases)
                return carry

            lax.fori_loop(1 if isinstance(g, int) else 0, 32, one, 0, unroll=4)

        in_groups(group)
        got[me] = send[channel]

        def gates(m, carry):
            at = lanes(m, 256)
            gate[:, at] = sigmoid(jnp.dot(weights[n, 4], normed[:, at], preferred_element_type=F32))
            return carry

        lax.fori_loop(0, 8, gates, 0, unroll=4)

    def mix(n, send, got, before, back, target, phases):
        for g in range(4):
            source = (group_here - g) & 3
            await_phase(g, got, before)
            for zz in range(4):
                rr = row_of(source, zz)
                grouped = source * 128 + zz * 32
                for f in range(2):
                    start = rr * 32 if n == 0 and f == 1 else grouped
                    for m in range(4):
                        both = halves(got[rr * NC + 2 * m, f], got[rr * NC + 2 * m + 1, f])
                        for h in range(2):
                            to = pl.ds(pl.multiple_of(start + h * 16, 16), 16)
                            matrices[f, to, m * 128 : m * 128 + 128] = both[h]
            if n == 1:
                turned[:, lanes(source, 128)] = matrices[0, lanes(source, 128), :].T
        await_sends(send, before)

        def group(g):
            q = (group_here + g) & 3
            if n == 0:
                rows = [matrices[0, lanes(q * 4 + ((z + k) & 3), 32), :] for k in range(4)]
            else:
                rows = [turned[lanes(row_of(q, (z + k) & 3), 32), :] for k in range(4)]
            left = jnp.concatenate(rows, axis=0)
            if n == 0:
                product = lax.dot_general(
                    left, matrices[1], (((1,), (1,)), ((), ())), preferred_element_type=F32
                )
            else:
                product = jnp.dot(left, matrices[1], preferred_element_type=F32)
            for k in range(4):
                zz = (z + k) & 3
                rr = row_of(q, zz)
                for m in range(4):
                    s = slice(m * 128, m * 128 + 128)
                    both = halves(product[k * 32 : k * 32 + 16, s], product[k * 32 + 16 : k * 32 + 32, s])
                    for h in range(2):
                        back[rr * NC + 2 * m + h] = both[h].astype(BF)
                for i in range(NC):
                    if k == 0 and i == 0 and isinstance(g, int):
                        continue
                    cc = (c + i) & 7
                    send_one(g, zz, cc, rr, back.at[rr * NC + cc], target.at[channel], phases)

        in_groups(group)
        target[channel] = back[me]

    def finish(n, back, mixed, before):
        for g in range(4):
            source = (group_here - g) & 3
            await_phase(g, mixed, before)
            spread_l[lanes(source, 512), :] = mixed[lanes(source, 32)].astype(F32).reshape(512, 128)
        await_sends(back, before)

        def one(t2, carry):
            sides = []
            for k in range(2):
                sides.append(
                    jnp.concatenate(
                        [spread_l[pl.ds(b * 128 + t2 * 2 + k, 8, stride=16), :] for b in range(16)],
                        axis=0,
                    )
                )
            v = columns_normed(jnp.concatenate(sides, axis=1)).astype(BF)
            at = lanes(t2, 256)
            now = pair[:, at] + gate[:, at] * jnp.dot(finals[n], v, preferred_element_type=F32)
            if n == 0:
                pair[:, at] = now
                normed[:, at] = columns_normed(now).astype(BF)
            else:
                for k in range(2):
                    block = now[:, k * 128 : k * 128 + 128].T
                    pair_in[t2 * 2 + k] = block[:64]
                    pair_in[t2 * 2 + k + 16] = block[64:]
                for h in range(2):
                    part = pl.ds(t2 * 2 + h * 16, 2)
                    pltpu.make_async_copy(pair_in.at[part], result.at[part], lsem.at[0]).start()
            return carry

        lax.fori_loop(0, 8, one, 0, unroll=8)
        if n == 1:
            pltpu.make_async_copy(pair_in, result, lsem.at[0]).wait()

    for n, (send, got, back, target) in enumerate(
        ((send1, got1, back1, mix1), (send2, got2, back2, mix2))
    ):
        project(n, send, got, sems.at[2 * n])
        mix(n, send, got, sems.at[2 * n], back, target, sems.at[2 * n + 1])
        finish(n, back, target, sems.at[2 * n + 1])


def local(
    alignment,
    pair_state,
    alignment_factor_weight,
    outer_proj,
    outgoing_proj,
    outgoing_final,
    incoming_proj,
    incoming_final,
):
    vmem = pl.BlockSpec(memory_space=pltpu.VMEM)
    hbm = pl.BlockSpec(memory_space=pltpu.HBM)
    v = pltpu.VMEM
    exchanged = [
        v((128, 2, 16, 128), BF), v((128, 2, 16, 128), BF), v((128, 16, 128), BF), v((128, 16, 128), BF),
    ]
    return pl.pallas_call(
        kernel,
        out_shape=jax.ShapeDtypeStruct((32, 64, 128), F32),
        in_specs=[hbm] * 8,
        out_specs=hbm,
        scratch_shapes=[
            v((16, 4096), BF), v((64, 64), BF), v((32, 64, 128), F32), v((1024, 128), BF),
            v((128, 640), BF), v((128, 128), BF), v((128, 640), BF), v((128, 128), BF),
            v((2, 8, 16, 128), BF), v((256, 2048), BF), v((8, 256, 128), BF), v((1024, 256), BF),
            v((1024, 2048), BF), v((128, 2048), F32), v((128, 2048), BF),
            v((128, 2048), F32), v((2048, 128), F32), v((2048, 128), F32),
            v((128, 1024), BF), v((2, 5, 128, 128), BF), v((2, 128, 128), BF),
            v((2, 512, 512), BF), v((512, 512), BF), v((128, 512), F32),
            *exchanged, *exchanged,
            pltpu.SemaphoreType.DMA((8,)),
            pltpu.SemaphoreType.DMA((10,)),
            pltpu.SemaphoreType.DMA((2,)),
            pltpu.SemaphoreType.DMA((8,)),
            pltpu.SemaphoreType.DMA((4, 5)),
        ],
        compiler_params=pltpu.CompilerParams(
            collective_id=0, has_side_effects=True, vmem_limit_bytes=56 << 20
        ),
    )(
        alignment, alignment_factor_weight, pair_state, outer_proj,
        outgoing_proj, outgoing_final, incoming_proj, incoming_final,
    )


def solution(mesh):
    return jax.shard_map(
        local,
        mesh=mesh,
        in_specs=(P("row", "col"), P("row", "col", None), P(), P(), P(), P(), P(), P()),
        out_specs=P("row", "col", None),
        check_vma=False,
    )
```
